256 devices in a mesh: ctx: 128 (over z, y, x_hi, core), kvh: 2 (over x_lo).
Axes of the slice: x: 4 (x_hi: 2, x_lo: 2; x = x_hi * 2 + x_lo), y: 4, z: 8, core: 2. Of those that a mesh axis runs over, the one named last changes fastest.
Arguments:
- queries: bfloat16 [256, 4, 16, 128], P('ctx', 'kvh'), may hold values from -12 to 12
- k_cache: bfloat16 [196608, 4, 128], P('ctx', 'kvh'), may hold values from -8 to 8
- v_cache: bfloat16 [196608, 4, 128], P('ctx', 'kvh'), may hold values from -6 to 6
- block_owner: int32 [1536], P('ctx'), may hold values from 0 to 1535, each once
- cached_lens: int32 [4], replicated, may hold values from 1 to 49086, as said below
- new_counts: int32 [4], replicated, may hold values from 1 to 64, 192 in all
Outputs:
- attended: bfloat16 [256, 64, 128], P(('ctx', 'kvh'))
The draws below stay inside these ranges and needn't reach their ends.
Inputs may be any that keep to these rules, and one draw needn't show every extreme that they name: `block_owner`: each sequence's new tokens follow its cached tokens; every logical block is held by exactly one physical block. `cached_lens`: one sequence has exactly 49086 cached tokens; the four add up to 65448. `new_counts`: one sequence has exactly 64 new tokens; the four add up to 192.
All inputs are finite; a program needn't handle non-finite values.
Results may differ from the reference program's by a relative error of at most 0.013.
Values may be sent and summed in bfloat16 or wider, within the bound.
No kernel may reach another device: no remote copies, remote signals or barrier semaphores. Data moves between devices by JAX's collectives and lax.ppermute only.
A program may use at most 64 MiB of HBM per device.

```python
import math
import jax
import jax.numpy as jnp
import numpy as np

SEQS = 4
KVH = 4
GROUP = 16
HD = 128
BLOCK = 128
NEWT = 256
QLEN = 64
NBLK = 1536
SLOTS = 196608
MEAN = 16362


def draw_queries(key, part):
    key = jax.random.fold_in(key, 11)
    first_key = jax.random.fold_in(key, 0)
    values = jax.random.truncated_normal(first_key, -6.0, 6.0, (NEWT, KVH, GROUP, HD), jnp.float32)
    return values.astype(jnp.bfloat16)


def draw_k_cache(key, part):
    key = jax.random.fold_in(key, 12)
    first_key = jax.random.fold_in(key, 0)
    values = jax.random.truncated_normal(first_key, -6.0, 6.0, (SLOTS, KVH, HD), jnp.float32)
    return values.astype(jnp.bfloat16)


def draw_cached_lens(key, part):
    key = jax.random.fold_in(key, 13)
    first_key, second_key, third_key = jax.random.split(key, 3)
    first = jax.random.randint(first_key, (), 1, MEAN - 1, dtype=jnp.int32)
    second = jax.random.randint(second_key, (), 1, MEAN - first, dtype=jnp.int32)
    third = MEAN - first - second
    values = jnp.stack([jnp.int32(3 * MEAN), first, second, third]).astype(jnp.int32)
    return jax.random.permutation(third_key, values)


def shard_levels(key, shape, cuts, smallest, top_value):
    gain = 1.0
    for dim, parts in cuts:
        heights = jax.random.uniform(jax.random.fold_in(jax.random.fold_in(key, 6), dim), (parts,), jnp.float32, smallest / len(cuts), top_value / len(cuts))
        gain = gain * jnp.repeat(jnp.exp(heights), shape[dim] // parts).reshape((-1,) + (1,) * (len(shape) - 1 - dim))
    return gain


def length_profile(count, total, most, slope):
    loads = [(1 << 20) // math.isqrt(standing ** slope) + 1 for standing in range(2, count + 1)]
    rest, holding = total - most - (count - 1), [1] * (count - 1)
    while rest > 0:
        candidates = [i for i in range(count - 1) if holding[i] < most]
        pool, left = sum([loads[i] for i in candidates]), rest
        for i in candidates:
            more = min(most - holding[i], max(1, left * loads[i] // pool), rest)
            holding[i] = holding[i] + more
            rest = rest - more
    return np.array([most] + holding)


def uneven_parts(own_key, number_of, total, reach, slope):
    if number_of == 2:
        one = jax.random.randint(own_key, (), max(1, total - reach), min(reach, total - 1) + 1)
        return jnp.stack([one, total - one])
    lengths = jnp.asarray(length_profile(number_of, total, reach, slope), jnp.int32)
    couples = (number_of - 1) // 2
    giver, receiver = lengths[1:1 + 2 * couples:2], lengths[2:2 + 2 * couples:2]
    room = jnp.minimum(giver - 1, reach - receiver)
    shifted = jax.random.randint(jax.random.fold_in(own_key, 1), (couples,), 0, 1 << 20) % (room + 1)
    lengths = lengths.at[1:1 + 2 * couples:2].set(giver - shifted).at[2:2 + 2 * couples:2].set(receiver + shifted)
    return lengths[jax.random.permutation(jax.random.fold_in(own_key, 2), number_of)]


def normal_values(key, shape, scale, limit, shards=(), kind=jnp.bfloat16):
    entries = scale * jax.random.normal(key, shape, jnp.float32)
    if shards:
        entries = entries * shard_levels(key, shape, shards, -0.22, 0.18)
    return jnp.clip(entries, -limit, limit).astype(kind)


def setup_inputs(seed: int = 0) -> dict:
    splits = jax.random.split(jax.random.key(seed), 7)
    return {
        "queries": draw_queries(jax.random.fold_in(splits[6], 71), 0),
        "k_cache": draw_k_cache(jax.random.fold_in(splits[6], 71), 0),
        "v_cache": normal_values(splits[2], (SLOTS, KVH, HD), 1.0, 6.0, ((0, 128), (1, 2))),
        "block_owner": jax.random.permutation(splits[3], NBLK).astype(jnp.int32),
        "cached_lens": draw_cached_lens(jax.random.fold_in(splits[6], 71), 0),
        "new_counts": uneven_parts(splits[5], SEQS, 3 * QLEN, QLEN, 0).astype(jnp.int32),
    }


def reference(queries, k_cache, v_cache, block_owner, cached_lens, new_counts):
    block_count = block_owner.shape[0]
    blocks_per_seq = block_count // SEQS
    inverse = jnp.zeros((block_count,), jnp.int32).at[block_owner].set(jnp.arange(block_count, dtype=jnp.int32))
    score_scale = HD ** -0.5
    seq_length = blocks_per_seq * BLOCK
    key_positions = jnp.arange(seq_length, dtype=jnp.int32)
    results = []
    for sequence in range(SEQS):
        blocks = inverse[sequence * blocks_per_seq:(sequence + 1) * blocks_per_seq]
        slots = (blocks[:, None] * BLOCK + jnp.arange(BLOCK, dtype=jnp.int32)[None, :]).reshape(-1)
        within = jnp.arange(QLEN, dtype=jnp.int32)
        query_pos = cached_lens[sequence] + within
        usable = within < new_counts[sequence]
        visible = (key_positions[None, :] <= query_pos[:, None]) & usable[:, None]
        shown = visible[:, None, :]
        query_rows = queries[sequence * QLEN:(sequence + 1) * QLEN].astype(jnp.float32)
        per_head = []
        for kv_head in range(KVH):
            keys = k_cache[slots, kv_head].astype(jnp.float32)
            values = v_cache[slots, kv_head].astype(jnp.float32)
            scores = jnp.einsum("qgd,kd->qgk", query_rows[:, kv_head], keys) * score_scale
            maxima = jnp.max(jnp.where(shown, scores, -1e30), axis=-1)
            weights = jnp.where(shown, jnp.exp(scores - maxima[..., None]), 0.0)
            sums = jnp.sum(weights, axis=-1)
            rounded = weights.astype(jnp.bfloat16).astype(jnp.float32)
            context = jnp.einsum("qgk,kd->qgd", rounded, values)
            output = context / jnp.where(sums > 0.0, sums, 1.0)[..., None]
            output = jnp.where(usable[:, None, None], output, 0.0)
            per_head.append(output)
        results.append(jnp.stack(per_head, axis=1))
    whole = jnp.concatenate(results, axis=0)
    return whole.reshape(NEWT, KVH * GROUP, HD).astype(jnp.bfloat16)
```

```python
import functools

import jax
import jax.numpy as jnp
from jax import lax
from jax.experimental import pallas as pl
from jax.experimental.pallas import tpu as pltpu
from jax.sharding import Mesh, PartitionSpec as P

LOG2E = 1.4426950408889634
FLOOR = -1e29
MASKED = -1e30

BLK = 128
OWN = 12
BOTH = 2 * OWN
HEADS = 2
GROUP = 16
HD = 128
SEQS = 4
UNITS = SEQS * HEADS
MSG = HD + 8
BEYOND = 1 << 20
PAIRS = (BOTH + SEQS) // 2
WIDE = HEADS * BLK
LAST = HEADS * GROUP + 8
SMEM = pl.BlockSpec(memory_space=pltpu.SMEM)
VMEM = pl.BlockSpec(memory_space=pltpu.VMEM)
COST = pl.CostEstimate(flops=1_000_000_000, bytes_accessed=4 << 20, transcendentals=0)


def split3(x):
    hi = x.astype(jnp.bfloat16).astype(jnp.float32)
    rest = x - hi
    mid = rest.astype(jnp.bfloat16).astype(jnp.float32)
    return hi, mid, rest - mid


def prep_kernel(own_ids, peer_ids, cached, counts, k0, k1, v0, v1, list_ref, k_ref, v_ref):
    blocks_per_seq = (BOTH * 64) // SEQS
    found = []
    for b in range(BOTH):
        ident = own_ids[b] if b < OWN else peer_ids[b - OWN]
        s = sum((ident >= n * blocks_per_seq).astype(jnp.int32) for n in range(1, SEQS))
        number = ident - s * blocks_per_seq
        found.append((s, number, number * BLK <= cached[s] + counts[s] - 1))
    at = []
    end = jnp.int32(0)
    for n in range(SEQS):
        at.append(end)
        here = sum(((s == n) & hit).astype(jnp.int32) for s, _, hit in found)
        end = end + ((here + 1) & -2)
    pairs = ((end >> 1) + 1) & -2
    for e in range(2 * PAIRS):
        list_ref[0, e] = 0
        list_ref[1, e] = BEYOND
    for p in range(PAIRS):
        list_ref[2, p] = sum((p >= (at[n] >> 1)).astype(jnp.int32) for n in range(1, SEQS))
    for n in range(SEQS):
        list_ref[2, 16 + n] = at[n]
    for b, (s, number, hit) in enumerate(found):
        e = jnp.where(hit, list_ref[2, 16 + s], 31)
        list_ref[0, e] = b
        list_ref[1, e] = number
        list_ref[2, 16 + s] += hit.astype(jnp.int32)
    list_ref[2, 31] = pairs

    def place_pair(p, _):
        for i in range(2):
            here = slice(i * BLK, (i + 1) * BLK)
            b = list_ref[0, 2 * p + i]

            def put(k_from, v_from, first):
                rows = pl.ds(pl.multiple_of((b - first) * BLK, BLK), BLK)
                for h in range(HEADS):
                    k_ref[p, h, here, :] = k_from[h, rows, :]
                    v_ref[p, h, :, here] = jnp.transpose(v_from[h, rows, :])

            pl.when(b < OWN)(lambda: put(k0, v0, 0))
            pl.when(b >= OWN)(lambda: put(k1, v1, OWN))
        return 0

    lax.fori_loop(0, pairs, place_pair, 0)


def attend_kernel(steps, *refs):
    n = len(steps)
    lists, cached, counts, place = refs[:4]
    q_refs, (k_ref, v_ref) = refs[4:4 + 2 * n], refs[4 + 2 * n:6 + 2 * n]
    out_refs, (m_ref, l_ref, acc_ref, t_ref) = refs[6 + 2 * n:6 + 3 * n], refs[6 + 3 * n:]
    rows = BLK * n
    lane = lax.broadcasted_iota(jnp.int32, (1, rows), 1)
    far = steps[0] if n == 1 else jnp.where(lane < BLK, steps[0], steps[1])
    within = (
        32 * ((lane >> 5) & 1)
        + 8 * ((place[1] + far) & 3)
        + 4 * (((lane >> 6) + place[2]) & 1)
        + 2 * place[3]
        + ((lane >> 4) & 1)
    )
    slot = lax.broadcasted_iota(jnp.int32, (BLK, rows), 0)
    scale = LOG2E * HD ** -0.5
    count = lists[2, 31]
    m_ref[...] = jnp.full(m_ref.shape, FLOOR, jnp.float32)
    l_ref[...] = jnp.zeros(l_ref.shape, jnp.float32)
    acc_ref[...] = jnp.zeros(acc_ref.shape, jnp.float32)

    def score(j, _):
        for p in (2 * j, 2 * j + 1):
            s = lists[2, p]
            qpos = jnp.where(within < counts[s], cached[s] + within, -1)
            for h in range(HEADS):
                unit = s * HEADS + h
                q = jnp.concatenate(
                    [r[pl.ds(2 * s, 2), :, h].reshape(BLK // 2, HD) for r in q_refs], axis=0
                )
                t = lax.dot_general(
                    k_ref[p, h], q, (((1,), (1,)), ((), ())), preferred_element_type=jnp.float32
                )
                top = None
                for i in range(2):
                    limit = qpos - lists[1, 2 * p + i] * BLK
                    part = jnp.where(slot <= limit, t[i * BLK:(i + 1) * BLK] * scale, MASKED)
                    t_ref[p, h, i * BLK:(i + 1) * BLK, :] = part
                    peak = jnp.max(part.reshape(BLK // 8, 8, rows), axis=0)
                    top = peak if top is None else jnp.maximum(top, peak)
                m_ref[unit] = jnp.maximum(m_ref[unit], top)
        return 0

    lax.fori_loop(0, count >> 1, score, 0)
    for unit in range(UNITS):
        m_ref[unit] = jnp.broadcast_to(
            jnp.max(m_ref[unit], axis=0, keepdims=True), (8, rows)
        )

    def weigh(j, _):
        for p in (2 * j, 2 * j + 1):
            s = lists[2, p]
            for h in range(HEADS):
                unit = s * HEADS + h
                w = jnp.exp2(t_ref[p, h].reshape(2 * BLK // 8, 8, rows) - m_ref[unit][None])
                l_ref[unit] += jnp.sum(w, axis=0)
                acc_ref[unit] += jnp.dot(
                    v_ref[p, h],
                    w.reshape(2 * BLK, rows).astype(jnp.bfloat16),
                    preferred_element_type=jnp.float32,
                )
        return 0

    lax.fori_loop(0, count >> 1, weigh, 0)

    for unit in range(UNITS):
        total = jnp.sum(l_ref[unit], axis=0, keepdims=True)
        some = total > 0.0
        safe = jnp.where(some, total, 1.0)
        lse = jnp.where(some, m_ref[unit, 0:1, :] + jnp.log(safe) * LOG2E, MASKED)
        ctx = acc_ref[unit] * (1.0 / safe)
        tail = jnp.concatenate(split3(lse) + (jnp.zeros((5, rows), jnp.float32),), axis=0)
        for i, out_ref in enumerate(out_refs):
            cols = slice(i * BLK, (i + 1) * BLK)
            there = slice(unit * BLK, (unit + 1) * BLK)
            out_ref[0:HD, there] = ctx[:, cols].astype(jnp.bfloat16)
            out_ref[HD:MSG, there] = tail[:, cols].astype(jnp.bfloat16)


def logs_of(ref, there):
    t = ref[HD:MSG, there].astype(jnp.float32)
    return t[0:1] + t[1:2] + t[2:3]


def join_kernel(in0, in1, out_ref):
    for unit in range(UNITS):
        there = slice(unit * BLK, (unit + 1) * BLK)
        logs = [logs_of(r, there) for r in (in0, in1)]
        top = jnp.maximum(*logs)
        w = [jnp.exp2(x - top) for x in logs]
        out_ref[0:HD, there] = (
            in0[0:HD, there].astype(jnp.float32) * w[0]
            + in1[0:HD, there].astype(jnp.float32) * w[1]
        )
        out_ref[HD:MSG, there] = jnp.concatenate(
            [top, w[0] + w[1], jnp.zeros((6, BLK), jnp.float32)], axis=0
        )


def fold_kernel(place, joined, in0, in1, out_ref):
    def dest(s, e):
        return 8 * s + 4 * ((e >> 1) & 1) + 2 * ((place[2] + (e >> 2)) & 1) + (e & 1)

    for s in range(SEQS):
        tails = []
        for h in range(HEADS):
            unit = s * HEADS + h
            there = slice(unit * BLK, (unit + 1) * BLK)
            logs = [joined[HD:HD + 1, there], logs_of(in0, there), logs_of(in1, there)]
            top = functools.reduce(jnp.maximum, logs)
            w = [jnp.exp2(x - top) for x in logs]
            total = joined[HD + 1:HD + 2, there] * w[0] + w[1] + w[2]
            inv = 1.0 / total
            ctx = (
                joined[0:HD, there] * (w[0] * inv)
                + in0[0:HD, there].astype(jnp.float32) * (w[1] * inv)
                + in1[0:HD, there].astype(jnp.float32) * (w[2] * inv)
            )
            ctx = jnp.transpose(ctx).astype(jnp.bfloat16)
            for e in range(8):
                out_ref[dest(s, e), h * GROUP:(h + 1) * GROUP, :] = ctx[e * GROUP:(e + 1) * GROUP]
            tails.extend(split3(top + jnp.log(total) * LOG2E))
        tail = jnp.concatenate(tails + [jnp.zeros((2, BLK), jnp.float32)], axis=0)
        for e in range(8):
            turned = tail if e == 0 else pltpu.roll(tail, BLK - GROUP * e, 1)
            out_ref[dest(s, e), 32:LAST, :] = turned.astype(jnp.bfloat16)


def finish_kernel(in_ref, out_ref):
    for kvh in range(2):
        sources = [2 * n + kvh for n in range(16)]
        t = jnp.concatenate(
            [in_ref[n, 32:LAST, :].astype(jnp.float32) for n in sources], axis=0
        )
        t = jnp.transpose(t)[0:GROUP]
        cols = t + pltpu.roll(t, BLK - 1, 1) + pltpu.roll(t, BLK - 2, 1)
        for h in range(HEADS):
            logs = []
            for n in range(16):
                at = n * 8 + 3 * h
                logs.append(jnp.broadcast_to(cols[:, at:at + 1], (GROUP, HD)))
            top = functools.reduce(jnp.maximum, logs)
            total = jnp.zeros((GROUP, HD), jnp.float32)
            ctx = jnp.zeros((GROUP, HD), jnp.float32)
            for n in range(16):
                w = jnp.exp2(logs[n] - top)
                total = total + w
                ctx = ctx + w * in_ref[
                    sources[n], h * GROUP:(h + 1) * GROUP, :
                ].astype(jnp.float32)
            first = kvh * 32 + h * GROUP
            out_ref[0, first:first + GROUP, :] = (ctx / total).astype(jnp.bfloat16)


def turn(x, axis, size, step):
    return lax.ppermute(x, axis, [((i + step) % size, i) for i in range(size)])


def params(mib):
    return pltpu.CompilerParams(vmem_limit_bytes=mib << 20)


def per_device(queries, k_cache, v_cache, block_owner, cached_lens, new_counts):
    k0, v0 = (x.reshape(OWN * WIDE, HD) for x in (k_cache, v_cache))
    k1, v1, ids = (turn(x, "core", 2, 1) for x in (k0, v0, block_owner))
    k0, k1, v0, v1 = (
        jnp.transpose(x.reshape(OWN * BLK, HEADS, HD), (1, 0, 2)) for x in (k0, k1, v0, v1)
    )
    place = jnp.stack([lax.axis_index(a).astype(jnp.int32) for a in ("z", "y", "xh", "core")])

    q = jnp.broadcast_to(queries[None], (8,) + queries.shape)
    q = lax.all_to_all(q, "z", split_axis=0, concat_axis=0, tiled=True)
    lists, k, v = pl.pallas_call(
        prep_kernel,
        out_shape=[
            jax.ShapeDtypeStruct((3, 32), jnp.int32),
            jax.ShapeDtypeStruct((PAIRS, HEADS, 2 * BLK, HD), jnp.bfloat16),
            jax.ShapeDtypeStruct((PAIRS, HEADS, HD, 2 * BLK), jnp.bfloat16),
        ],
        in_specs=[SMEM] * 4 + [VMEM] * 4,
        out_specs=[SMEM, VMEM, VMEM],
        compiler_params=params(8),
        cost_estimate=COST,
        name="prep",
    )(block_owner, ids, cached_lens, new_counts, k0, k1, v0, v1)

    q, lists, k, v = lax.optimization_barrier((q, lists, k, v))
    both = [q, turn(q, "xh", 2, 1)]
    near, back = ([turn(x, "y", 4, n) for x in both] for n in (1, 3))
    qs = [both, near, [turn(near[0], "y", 4, 1), turn(back[1], "y", 4, 3)], back]

    def attend(place, *steps):
        n = len(steps)
        rows = n * BLK
        return pl.pallas_call(
            functools.partial(attend_kernel, steps),
            out_shape=[jax.ShapeDtypeStruct((MSG, 8 * BLK), jnp.bfloat16)] * n,
            in_specs=[SMEM] * 4 + [VMEM] * (2 * n + 2),
            out_specs=[VMEM] * n,
            scratch_shapes=[
                pltpu.VMEM((UNITS, 8, rows), jnp.float32),
                pltpu.VMEM((UNITS, 8, rows), jnp.float32),
                pltpu.VMEM((UNITS, HD, rows), jnp.float32),
                pltpu.VMEM((PAIRS, HEADS, 2 * BLK, rows), jnp.float32),
            ],
            compiler_params=params(12),
            cost_estimate=COST,
            name="attend" + "".join(map(str, steps)),
        )(lists, cached_lens, new_counts, place, *[x for i in steps for x in qs[i]], k, v)

    msg1, msg3 = attend(place, 1, 3)
    (msg2,) = attend(place, 2)
    (msg0,) = attend(place, 0)
    joined = pl.pallas_call(
        join_kernel,
        out_shape=jax.ShapeDtypeStruct((MSG, 8 * BLK), jnp.float32),
        in_specs=[VMEM] * 2,
        out_specs=VMEM,
        compiler_params=params(8),
        cost_estimate=COST,
        name="join",
    )(turn(msg1, "y", 4, -1), turn(msg3, "y", 4, -3))
    msg = pl.pallas_call(
        fold_kernel,
        out_shape=jax.ShapeDtypeStruct((32, LAST, HD), jnp.bfloat16),
        in_specs=[SMEM] + [VMEM] * 3,
        out_specs=VMEM,
        compiler_params=params(8),
        name="fold",
    )(place, joined, msg0, turn(msg2, "y", 4, -2))
    msg = lax.all_to_all(msg, ("z", "xh", "kvh"), split_axis=0, concat_axis=0, tiled=True)
    return pl.pallas_call(
        finish_kernel,
        out_shape=jax.ShapeDtypeStruct((1, 64, HD), jnp.bfloat16),
        in_specs=[VMEM],
        out_specs=VMEM,
        compiler_params=params(4),
        name="finish",
    )(msg)


def solution(mesh):
    split = Mesh(mesh.devices.reshape(8, 4, 2, 2, 2), ("z", "y", "xh", "core", "kvh"))
    ctx = ("z", "y", "xh", "core")
    in_specs = (
        P(ctx, "kvh", None, None),
        P(ctx, "kvh", None),
        P(ctx, "kvh", None),
        P(ctx),
        P(),
        P(),
    )
    return jax.shard_map(
        per_device,
        mesh=split,
        in_specs=in_specs,
        out_specs=P(ctx + ("kvh",), None, None),
        check_vma=False,
    )
```

```python
import functools

import jax
import jax.numpy as jnp
from jax import lax
from jax.experimental import pallas as pl
from jax.experimental.pallas import tpu as pltpu
from jax.sharding import Mesh, PartitionSpec as P

LOG2E = 1.4426950408889634
FLOOR = -1e29
MASKED = -1e30

BLK = 128
OWN = 12
BOTH = 2 * OWN
HEADS = 2
GROUP = 16
HD = 128
SEQS = 4
UNITS = SEQS * HEADS
MSG = HD + 8
BEYOND = 1 << 20
PAIRS = (BOTH + SEQS) // 2
WIDE = HEADS * BLK
LAST = HEADS * GROUP + 8
SMEM = pl.BlockSpec(memory_space=pltpu.SMEM)
VMEM = pl.BlockSpec(memory_space=pltpu.VMEM)
COST = pl.CostEstimate(flops=1_000_000_000, bytes_accessed=4 << 20, transcendentals=0)


def split3(x):
    hi = x.astype(jnp.bfloat16).astype(jnp.float32)
    rest = x - hi
    mid = rest.astype(jnp.bfloat16).astype(jnp.float32)
    return hi, mid, rest - mid


def select_kernel(own_ids, peer_ids, cached, counts, list_ref):
    blocks_per_seq = (BOTH * 64) // SEQS
    found = []
    for b in range(BOTH):
        ident = own_ids[b] if b < OWN else peer_ids[b - OWN]
        s = sum((ident >= n * blocks_per_seq).astype(jnp.int32) for n in range(1, SEQS))
        number = ident - s * blocks_per_seq
        found.append((s, number, number * BLK <= cached[s] + counts[s] - 1))
    at = []
    end = jnp.int32(0)
    for n in range(SEQS):
        at.append(end)
        here = sum(((s == n) & hit).astype(jnp.int32) for s, _, hit in found)
        end = end + ((here + 1) & -2)
    pairs = ((end >> 1) + 1) & -2
    for e in range(2 * PAIRS):
        list_ref[0, e] = 0
        list_ref[1, e] = BEYOND
    for p in range(PAIRS):
        list_ref[2, p] = sum((p >= (at[n] >> 1)).astype(jnp.int32) for n in range(1, SEQS))
    for n in range(SEQS):
        list_ref[2, 16 + n] = at[n]
    for b, (s, number, hit) in enumerate(found):
        e = jnp.where(hit, list_ref[2, 16 + s], 31)
        list_ref[0, e] = b
        list_ref[1, e] = number
        list_ref[2, 16 + s] += hit.astype(jnp.int32)
    list_ref[2, 31] = pairs


def pack_kernel(lists, k0, k1, v0, v1, k_ref, v_ref):
    def place_pair(p, _):
        for i in range(2):
            here = slice(i * BLK, (i + 1) * BLK)
            b = lists[0, 2 * p + i]

            def put(k_from, v_from, first):
                rows = pl.ds(pl.multiple_of((b - first) * BLK, BLK), BLK)
                for h in range(HEADS):
                    k_ref[p, h, here, :] = k_from[h, rows, :]
                    v_ref[p, h, :, here] = jnp.transpose(v_from[h, rows, :])

            pl.when(b < OWN)(lambda: put(k0, v0, 0))
            pl.when(b >= OWN)(lambda: put(k1, v1, OWN))
        return 0

    lax.fori_loop(0, lists[2, 31], place_pair, 0)


def attend_kernel(steps, *refs):
    n = len(steps)
    lists, cached, counts, place = refs[:4]
    q_refs, (k_ref, v_ref) = refs[4:4 + 2 * n], refs[4 + 2 * n:6 + 2 * n]
    out_refs, (m_ref, l_ref, acc_ref, t_ref) = refs[6 + 2 * n:6 + 3 * n], refs[6 + 3 * n:]
    rows = BLK * n
    lane = lax.broadcasted_iota(jnp.int32, (1, rows), 1)
    far = steps[0] if n == 1 else jnp.where(lane < BLK, steps[0], steps[1])
    within = (
        32 * ((lane >> 5) & 1)
        + 8 * ((place[1] + far) & 3)
        + 4 * (((lane >> 6) + place[2]) & 1)
        + 2 * place[3]
        + ((lane >> 4) & 1)
    )
    slot = lax.broadcasted_iota(jnp.int32, (BLK, rows), 0)
    scale = LOG2E * HD ** -0.5
    count = lists[2, 31]
    m_ref[...] = jnp.full(m_ref.shape, FLOOR, jnp.float32)
    l_ref[...] = jnp.zeros(l_ref.shape, jnp.float32)
    acc_ref[...] = jnp.zeros(acc_ref.shape, jnp.float32)

    def score(j, _):
        for p in (2 * j, 2 * j + 1):
            s = lists[2, p]
            qpos = jnp.where(within < counts[s], cached[s] + within, -1)
            for h in range(HEADS):
                unit = s * HEADS + h
                q = jnp.concatenate(
                    [r[pl.ds(2 * s, 2), :, h].reshape(BLK // 2, HD) for r in q_refs], axis=0
                )
                t = lax.dot_general(
                    k_ref[p, h], q, (((1,), (1,)), ((), ())), preferred_element_type=jnp.float32
                )
                top = None
                for i in range(2):
                    limit = qpos - lists[1, 2 * p + i] * BLK
                    part = jnp.where(slot <= limit, t[i * BLK:(i + 1) * BLK] * scale, MASKED)
                    t_ref[p, h, i * BLK:(i + 1) * BLK, :] = part
                    peak = jnp.max(part.reshape(BLK // 8, 8, rows), axis=0)
                    top = peak if top is None else jnp.maximum(top, peak)
                m_ref[unit] = jnp.maximum(m_ref[unit], top)
        return 0

    lax.fori_loop(0, count >> 1, score, 0)
    for unit in range(UNITS):
        m_ref[unit] = jnp.broadcast_to(
            jnp.max(m_ref[unit], axis=0, keepdims=True), (8, rows)
        )

    def weigh(j, _):
        for p in (2 * j, 2 * j + 1):
            s = lists[2, p]
            for h in range(HEADS):
                unit = s * HEADS + h
                w = jnp.exp2(t_ref[p, h].reshape(2 * BLK // 8, 8, rows) - m_ref[unit][None])
                l_ref[unit] += jnp.sum(w, axis=0)
                acc_ref[unit] += jnp.dot(
                    v_ref[p, h],
                    w.reshape(2 * BLK, rows).astype(jnp.bfloat16),
                    preferred_element_type=jnp.float32,
                )
        return 0

    lax.fori_loop(0, count >> 1, weigh, 0)

    for unit in range(UNITS):
        total = jnp.sum(l_ref[unit], axis=0, keepdims=True)
        some = total > 0.0
        safe = jnp.where(some, total, 1.0)
        lse = jnp.where(some, m_ref[unit, 0:1, :] + jnp.log(safe) * LOG2E, MASKED)
        ctx = acc_ref[unit] * (1.0 / safe)
        tail = jnp.concatenate(split3(lse) + (jnp.zeros((5, rows), jnp.float32),), axis=0)
        for i, out_ref in enumerate(out_refs):
            cols = slice(i * BLK, (i + 1) * BLK)
            there = slice(unit * BLK, (unit + 1) * BLK)
            out_ref[0:HD, there] = ctx[:, cols].astype(jnp.bfloat16)
            out_ref[HD:MSG, there] = tail[:, cols].astype(jnp.bfloat16)


def logs_of(ref, there):
    t = ref[HD:MSG, there].astype(jnp.float32)
    return t[0:1] + t[1:2] + t[2:3]


def join_kernel(in0, in1, out_ref):
    for unit in range(UNITS):
        there = slice(unit * BLK, (unit + 1) * BLK)
        logs = [logs_of(r, there) for r in (in0, in1)]
        top = jnp.maximum(*logs)
        w = [jnp.exp2(x - top) for x in logs]
        out_ref[0:HD, there] = (
            in0[0:HD, there].astype(jnp.float32) * w[0]
            + in1[0:HD, there].astype(jnp.float32) * w[1]
        )
        out_ref[HD:MSG, there] = jnp.concatenate(
            [top, w[0] + w[1], jnp.zeros((6, BLK), jnp.float32)], axis=0
        )


def fold_kernel(place, joined, in0, in1, out_ref):
    def dest(s, e):
        return 8 * s + 4 * ((e >> 1) & 1) + 2 * ((place[2] + (e >> 2)) & 1) + (e & 1)

    for s in range(SEQS):
        tails = []
        for h in range(HEADS):
            unit = s * HEADS + h
            there = slice(unit * BLK, (unit + 1) * BLK)
            logs = [joined[HD:HD + 1, there], logs_of(in0, there), logs_of(in1, there)]
            top = functools.reduce(jnp.maximum, logs)
            w = [jnp.exp2(x - top) for x in logs]
            total = joined[HD + 1:HD + 2, there] * w[0] + w[1] + w[2]
            inv = 1.0 / total
            ctx = (
                joined[0:HD, there] * (w[0] * inv)
                + in0[0:HD, there].astype(jnp.float32) * (w[1] * inv)
                + in1[0:HD, there].astype(jnp.float32) * (w[2] * inv)
            )
            ctx = jnp.transpose(ctx).astype(jnp.bfloat16)
            for e in range(8):
                out_ref[dest(s, e), h * GROUP:(h + 1) * GROUP, :] = ctx[e * GROUP:(e + 1) * GROUP]
            tails.extend(split3(top + jnp.log(total) * LOG2E))
        tail = jnp.concatenate(tails + [jnp.zeros((2, BLK), jnp.float32)], axis=0)
        for e in range(8):
            turned = tail if e == 0 else pltpu.roll(tail, BLK - GROUP * e, 1)
            out_ref[dest(s, e), 32:LAST, :] = turned.astype(jnp.bfloat16)


def finish_kernel(in_ref, out_ref):
    for kvh in range(2):
        sources = [2 * n + kvh for n in range(16)]
        t = jnp.concatenate(
            [in_ref[n, 32:LAST, :].astype(jnp.float32) for n in sources], axis=0
        )
        t = jnp.transpose(t)[0:GROUP]
        cols = t + pltpu.roll(t, BLK - 1, 1) + pltpu.roll(t, BLK - 2, 1)
        for h in range(HEADS):
            logs = []
            for n in range(16):
                at = n * 8 + 3 * h
                logs.append(jnp.broadcast_to(cols[:, at:at + 1], (GROUP, HD)))
            top = functools.reduce(jnp.maximum, logs)
            total = jnp.zeros((GROUP, HD), jnp.float32)
            ctx = jnp.zeros((GROUP, HD), jnp.float32)
            for n in range(16):
                w = jnp.exp2(logs[n] - top)
                total = total + w
                ctx = ctx + w * in_ref[
                    sources[n], h * GROUP:(h + 1) * GROUP, :
                ].astype(jnp.float32)
            first = kvh * 32 + h * GROUP
            out_ref[0, first:first + GROUP, :] = (ctx / total).astype(jnp.bfloat16)


def turn(x, axis, size, step):
    return lax.ppermute(x, axis, [((i + step) % size, i) for i in range(size)])


def params(mib):
    return pltpu.CompilerParams(vmem_limit_bytes=mib << 20)


def per_device(queries, k_cache, v_cache, block_owner, cached_lens, new_counts):
    k0, v0 = (x.reshape(OWN * WIDE, HD) for x in (k_cache, v_cache))
    k1, v1, ids = (turn(x, "core", 2, 1) for x in (k0, v0, block_owner))
    k0, k1, v0, v1 = (
        jnp.transpose(x.reshape(OWN * BLK, HEADS, HD), (1, 0, 2)) for x in (k0, k1, v0, v1)
    )
    place = jnp.stack([lax.axis_index(a).astype(jnp.int32) for a in ("z", "y", "xh", "core")])

    lists = pl.pallas_call(
        select_kernel,
        out_shape=jax.ShapeDtypeStruct((3, 32), jnp.int32),
        in_specs=[SMEM] * 4,
        out_specs=SMEM,
        compiler_params=params(12),
        name="select",
    )(block_owner, ids, cached_lens, new_counts)

    q = jnp.broadcast_to(queries[None], (8,) + queries.shape)
    q = lax.all_to_all(q, "z", split_axis=0, concat_axis=0, tiled=True)
    q, lists = lax.optimization_barrier((q, lists))
    k, v = pl.pallas_call(
        pack_kernel,
        out_shape=[
            jax.ShapeDtypeStruct((PAIRS, HEADS, 2 * BLK, HD), jnp.bfloat16),
            jax.ShapeDtypeStruct((PAIRS, HEADS, HD, 2 * BLK), jnp.bfloat16),
        ],
        in_specs=[SMEM] + [VMEM] * 4,
        out_specs=[VMEM, VMEM],
        compiler_params=params(12),
        cost_estimate=COST,
        name="pack",
    )(lists, k0, k1, v0, v1)
    over, near, back, k, v = lax.optimization_barrier(
        (turn(q, "xh", 2, 1), turn(q, "y", 4, 1), turn(q, "y", 4, 3), k, v)
    )
    near, back = [near, turn(over, "y", 4, 1)], [back, turn(over, "y", 4, 3)]
    qs = [[q, over], near, [turn(near[0], "y", 4, 1), turn(back[1], "y", 4, 3)], back]

    def attend(place, *steps):
        n = len(steps)
        rows = n * BLK
        return pl.pallas_call(
            functools.partial(attend_kernel, steps),
            out_shape=[jax.ShapeDtypeStruct((MSG, 8 * BLK), jnp.bfloat16)] * n,
            in_specs=[SMEM] * 4 + [VMEM] * (2 * n + 2),
            out_specs=[VMEM] * n,
            scratch_shapes=[
                pltpu.VMEM((UNITS, 8, rows), jnp.float32),
                pltpu.VMEM((UNITS, 8, rows), jnp.float32),
                pltpu.VMEM((UNITS, HD, rows), jnp.float32),
                pltpu.VMEM((PAIRS, HEADS, 2 * BLK, rows), jnp.float32),
            ],
            compiler_params=params(12),
            cost_estimate=COST,
            name="attend" + "".join(map(str, steps)),
        )(lists, cached_lens, new_counts, place, *[x for i in steps for x in qs[i]], k, v)

    msg1, msg3 = attend(place, 1, 3)
    (msg2,) = attend(place, 2)
    (msg0,) = attend(place, 0)
    joined = pl.pallas_call(
        join_kernel,
        out_shape=jax.ShapeDtypeStruct((MSG, 8 * BLK), jnp.float32),
        in_specs=[VMEM] * 2,
        out_specs=VMEM,
        compiler_params=params(12),
        cost_estimate=COST,
        name="join",
    )(turn(msg1, "y", 4, -1), turn(msg3, "y", 4, -3))
    msg = pl.pallas_call(
        fold_kernel,
        out_shape=jax.ShapeDtypeStruct((32, LAST, HD), jnp.bfloat16),
        in_specs=[SMEM] + [VMEM] * 3,
        out_specs=VMEM,
        compiler_params=params(12),
        name="fold",
    )(place, joined, msg0, turn(msg2, "y", 4, -2))
    msg = lax.all_to_all(msg, ("z", "xh", "kvh"), split_axis=0, concat_axis=0, tiled=True)
    return pl.pallas_call(
        finish_kernel,
        out_shape=jax.ShapeDtypeStruct((1, 64, HD), jnp.bfloat16),
        in_specs=[VMEM],
        out_specs=VMEM,
        compiler_params=params(12),
        name="finish",
    )(msg)


def solution(mesh):
    split = Mesh(mesh.devices.reshape(8, 4, 2, 2, 2), ("z", "y", "xh", "core", "kvh"))
    ctx = ("z", "y", "xh", "core")
    in_specs = (
        P(ctx, "kvh", None, None),
        P(ctx, "kvh", None),
        P(ctx, "kvh", None),
        P(ctx),
        P(),
        P(),
    )
    return jax.shard_map(
        per_device,
        mesh=split,
        in_specs=in_specs,
        out_specs=P(ctx + ("kvh",), None, None),
        check_vma=False,
    )
```

```python
import functools

import jax
import jax.numpy as jnp
from jax import lax
from jax.experimental import pallas as pl
from jax.experimental.pallas import tpu as pltpu
from jax.sharding import Mesh, PartitionSpec as P

LOG2E = 1.4426950408889634
FLOOR = -1e29
MASKED = -1e30

BLK = 128
OWN = 12
BOTH = 2 * OWN
HEADS = 2
GROUP = 16
HD = 128
SEQS = 4
UNITS = SEQS * HEADS
MSG = HD + 8
BEYOND = 1 << 20
PAIRS = (BOTH + SEQS) // 2
WIDE = HEADS * BLK
LAST = HEADS * GROUP + 8
SMEM = pl.BlockSpec(memory_space=pltpu.SMEM)
VMEM = pl.BlockSpec(memory_space=pltpu.VMEM)
COST = pl.CostEstimate(flops=1_000_000_000, bytes_accessed=4 << 20, transcendentals=0)


def split3(x):
    hi = x.astype(jnp.bfloat16).astype(jnp.float32)
    rest = x - hi
    mid = rest.astype(jnp.bfloat16).astype(jnp.float32)
    return hi, mid, rest - mid


def select_kernel(own_ids, peer_ids, cached, counts, list_ref):
    blocks_per_seq = (BOTH * 64) // SEQS
    found = []
    for b in range(BOTH):
        ident = own_ids[b] if b < OWN else peer_ids[b - OWN]
        s = sum((ident >= n * blocks_per_seq).astype(jnp.int32) for n in range(1, SEQS))
        number = ident - s * blocks_per_seq
        found.append((s, number, number * BLK <= cached[s] + counts[s] - 1))
    at = []
    end = jnp.int32(0)
    for n in range(SEQS):
        at.append(end)
        here = sum(((s == n) & hit).astype(jnp.int32) for s, _, hit in found)
        end = end + ((here + 1) & -2)
    pairs = ((end >> 1) + 1) & -2
    for e in range(2 * PAIRS):
        list_ref[0, e] = 0
        list_ref[1, e] = BEYOND
    for p in range(PAIRS):
        list_ref[2, p] = sum((p >= (at[n] >> 1)).astype(jnp.int32) for n in range(1, SEQS))
    for n in range(SEQS):
        list_ref[2, 16 + n] = at[n]
    for b, (s, number, hit) in enumerate(found):
        e = jnp.where(hit, list_ref[2, 16 + s], 31)
        list_ref[0, e] = b
        list_ref[1, e] = number
        list_ref[2, 16 + s] += hit.astype(jnp.int32)
    list_ref[2, 31] = pairs


def pack_kernel(lists, k0, k1, v0, v1, k_ref, v_ref):
    def place_pair(p, _):
        for i in range(2):
            here = slice(i * BLK, (i + 1) * BLK)
            b = lists[0, 2 * p + i]

            def put(k_from, v_from, first):
                rows = pl.ds(pl.multiple_of((b - first) * BLK, BLK), BLK)
                for h in range(HEADS):
                    k_ref[p, h, here, :] = k_from[h, rows, :]
                    v_ref[p, h, :, here] = jnp.transpose(v_from[h, rows, :])

            pl.when(b < OWN)(lambda: put(k0, v0, 0))
            pl.when(b >= OWN)(lambda: put(k1, v1, OWN))
        return 0

    lax.fori_loop(0, lists[2, 31], place_pair, 0)


def attend_kernel(steps, *refs):
    n = len(steps)
    lists, cached, counts = refs[:3]
    q_refs, (k_ref, v_ref) = refs[3:3 + 2 * n], refs[3 + 2 * n:5 + 2 * n]
    out_refs, (m_ref, l_ref, acc_ref, t_ref) = refs[5 + 2 * n:5 + 3 * n], refs[5 + 3 * n:]
    rows = BLK * n
    lane = lax.broadcasted_iota(jnp.int32, (1, rows), 1)
    far = steps[0] if n == 1 else jnp.where(lane < BLK, steps[0], steps[1])
    within = (
        32 * ((lane >> 5) & 1)
        + 8 * ((lax.axis_index("y") + far) & 3)
        + 4 * (((lane >> 6) + lax.axis_index("xh")) & 1)
        + 2 * lax.axis_index("core")
        + ((lane >> 4) & 1)
    )
    slot = lax.broadcasted_iota(jnp.int32, (BLK, rows), 0)
    scale = LOG2E * HD ** -0.5
    count = lists[2, 31]
    m_ref[...] = jnp.full(m_ref.shape, FLOOR, jnp.float32)
    l_ref[...] = jnp.zeros(l_ref.shape, jnp.float32)
    acc_ref[...] = jnp.zeros(acc_ref.shape, jnp.float32)

    def score(j, _):
        for p in (2 * j, 2 * j + 1):
            s = lists[2, p]
            qpos = jnp.where(within < counts[s], cached[s] + within, -1)
            for h in range(HEADS):
                unit = s * HEADS + h
                q = jnp.concatenate(
                    [r[pl.ds(2 * s, 2), :, h].reshape(BLK // 2, HD) for r in q_refs], axis=0
                )
                t = lax.dot_general(
                    k_ref[p, h], q, (((1,), (1,)), ((), ())), preferred_element_type=jnp.float32
                )
                top = None
                for i in range(2):
                    limit = qpos - lists[1, 2 * p + i] * BLK
                    part = jnp.where(slot <= limit, t[i * BLK:(i + 1) * BLK] * scale, MASKED)
                    t_ref[p, h, i * BLK:(i + 1) * BLK, :] = part
                    peak = jnp.max(part.reshape(BLK // 8, 8, rows), axis=0)
                    top = peak if top is None else jnp.maximum(top, peak)
                m_ref[unit] = jnp.maximum(m_ref[unit], top)
        return 0

    lax.fori_loop(0, count >> 1, score, 0)
    for unit in range(UNITS):
        m_ref[unit] = jnp.broadcast_to(
            jnp.max(m_ref[unit], axis=0, keepdims=True), (8, rows)
        )

    def weigh(j, _):
        for p in (2 * j, 2 * j + 1):
            s = lists[2, p]
            for h in range(HEADS):
                unit = s * HEADS + h
                w = jnp.exp2(t_ref[p, h].reshape(2 * BLK // 8, 8, rows) - m_ref[unit][None])
                l_ref[unit] += jnp.sum(w, axis=0)
                acc_ref[unit] += jnp.dot(
                    v_ref[p, h],
                    w.reshape(2 * BLK, rows).astype(jnp.bfloat16),
                    preferred_element_type=jnp.float32,
                )
        return 0

    lax.fori_loop(0, count >> 1, weigh, 0)

    for unit in range(UNITS):
        total = jnp.sum(l_ref[unit], axis=0, keepdims=True)
        some = total > 0.0
        safe = jnp.where(some, total, 1.0)
        lse = jnp.where(some, m_ref[unit, 0:1, :] + jnp.log(safe) * LOG2E, MASKED)
        ctx = acc_ref[unit] * (1.0 / safe)
        tail = jnp.concatenate(split3(lse) + (jnp.zeros((5, rows), jnp.float32),), axis=0)
        for i, out_ref in enumerate(out_refs):
            cols = slice(i * BLK, (i + 1) * BLK)
            there = slice(unit * BLK, (unit + 1) * BLK)
            out_ref[0:HD, there] = ctx[:, cols].astype(jnp.bfloat16)
            out_ref[HD:MSG, there] = tail[:, cols].astype(jnp.bfloat16)


def logs_of(ref, there):
    t = ref[HD:MSG, there].astype(jnp.float32)
    return t[0:1] + t[1:2] + t[2:3]


def join_kernel(in0, in1, out_ref):
    for unit in range(UNITS):
        there = slice(unit * BLK, (unit + 1) * BLK)
        logs = [logs_of(r, there) for r in (in0, in1)]
        top = jnp.maximum(*logs)
        w = [jnp.exp2(x - top) for x in logs]
        out_ref[0:HD, there] = (
            in0[0:HD, there].astype(jnp.float32) * w[0]
            + in1[0:HD, there].astype(jnp.float32) * w[1]
        )
        out_ref[HD:MSG, there] = jnp.concatenate(
            [top, w[0] + w[1], jnp.zeros((6, BLK), jnp.float32)], axis=0
        )


def fold_kernel(joined, in0, in1, out_ref):
    def dest(s, e):
        return 8 * s + 4 * ((e >> 1) & 1) + 2 * ((lax.axis_index("xh") + (e >> 2)) & 1) + (e & 1)

    for s in range(SEQS):
        tails = []
        for h in range(HEADS):
            unit = s * HEADS + h
            there = slice(unit * BLK, (unit + 1) * BLK)
            logs = [joined[HD:HD + 1, there], logs_of(in0, there), logs_of(in1, there)]
            top = functools.reduce(jnp.maximum, logs)
            w = [jnp.exp2(x - top) for x in logs]
            total = joined[HD + 1:HD + 2, there] * w[0] + w[1] + w[2]
            inv = 1.0 / total
            ctx = (
                joined[0:HD, there] * (w[0] * inv)
                + in0[0:HD, there].astype(jnp.float32) * (w[1] * inv)
                + in1[0:HD, there].astype(jnp.float32) * (w[2] * inv)
            )
            ctx = jnp.transpose(ctx).astype(jnp.bfloat16)
            for e in range(8):
                out_ref[dest(s, e), h * GROUP:(h + 1) * GROUP, :] = ctx[e * GROUP:(e + 1) * GROUP]
            tails.extend(split3(top + jnp.log(total) * LOG2E))
        tail = jnp.concatenate(tails + [jnp.zeros((2, BLK), jnp.float32)], axis=0)
        for e in range(8):
            turned = tail if e == 0 else pltpu.roll(tail, BLK - GROUP * e, 1)
            out_ref[dest(s, e), 32:LAST, :] = turned.astype(jnp.bfloat16)


def finish_kernel(in_ref, out_ref):
    for kvh in range(2):
        sources = [2 * n + kvh for n in range(16)]
        t = jnp.concatenate(
            [in_ref[n, 32:LAST, :].astype(jnp.float32) for n in sources], axis=0
        )
        t = jnp.transpose(t)[0:GROUP]
        cols = t + pltpu.roll(t, BLK - 1, 1) + pltpu.roll(t, BLK - 2, 1)
        for h in range(HEADS):
            logs = []
            for n in range(16):
                at = n * 8 + 3 * h
                logs.append(jnp.broadcast_to(cols[:, at:at + 1], (GROUP, HD)))
            top = functools.reduce(jnp.maximum, logs)
            total = jnp.zeros((GROUP, HD), jnp.float32)
            ctx = jnp.zeros((GROUP, HD), jnp.float32)
            for n in range(16):
                w = jnp.exp2(logs[n] - top)
                total = total + w
                ctx = ctx + w * in_ref[
                    sources[n], h * GROUP:(h + 1) * GROUP, :
                ].astype(jnp.float32)
            first = kvh * 32 + h * GROUP
            out_ref[0, first:first + GROUP, :] = (ctx / total).astype(jnp.bfloat16)


def turn(x, axis, size, step):
    return lax.ppermute(x, axis, [((i + step) % size, i) for i in range(size)])


def params(mib):
    return pltpu.CompilerParams(vmem_limit_bytes=mib << 20)


def per_device(queries, k_cache, v_cache, block_owner, cached_lens, new_counts):
    k0, v0 = (x.reshape(OWN * WIDE, HD) for x in (k_cache, v_cache))
    k1, v1, ids = (turn(x, "core", 2, 1) for x in (k0, v0, block_owner))

    lists = pl.pallas_call(
        select_kernel,
        out_shape=jax.ShapeDtypeStruct((3, 32), jnp.int32),
        in_specs=[SMEM] * 4,
        out_specs=SMEM,
        compiler_params=params(12),
        name="select",
    )(block_owner, ids, cached_lens, new_counts)

    q = jnp.broadcast_to(queries[None], (8,) + queries.shape)
    q = lax.all_to_all(q, "z", split_axis=0, concat_axis=0, tiled=True)
    q, lists, *caches = lax.optimization_barrier((q, lists, k0, k1, v0, v1))
    k0, k1, v0, v1 = (
        jnp.transpose(x.reshape(OWN * BLK, HEADS, HD), (1, 0, 2)) for x in caches
    )
    k, v = pl.pallas_call(
        pack_kernel,
        out_shape=[
            jax.ShapeDtypeStruct((PAIRS, HEADS, 2 * BLK, HD), jnp.bfloat16),
            jax.ShapeDtypeStruct((PAIRS, HEADS, HD, 2 * BLK), jnp.bfloat16),
        ],
        in_specs=[SMEM] + [VMEM] * 4,
        out_specs=[VMEM, VMEM],
        compiler_params=params(12),
        cost_estimate=COST,
        name="pack",
    )(lists, k0, k1, v0, v1)
    over, near, back, k, v = lax.optimization_barrier(
        (turn(q, "xh", 2, 1), turn(q, "y", 4, 1), turn(q, "y", 4, 3), k, v)
    )
    near, back = [near, turn(over, "y", 4, 1)], [back, turn(over, "y", 4, 3)]
    qs = [[q, over], near, [turn(near[0], "y", 4, 1), turn(back[1], "y", 4, 3)], back]

    def attend(*steps):
        n = len(steps)
        rows = n * BLK
        return pl.pallas_call(
            functools.partial(attend_kernel, steps),
            out_shape=[jax.ShapeDtypeStruct((MSG, 8 * BLK), jnp.bfloat16)] * n,
            in_specs=[SMEM] * 3 + [VMEM] * (2 * n + 2),
            out_specs=[VMEM] * n,
            scratch_shapes=[
                pltpu.VMEM((UNITS, 8, rows), jnp.float32),
                pltpu.VMEM((UNITS, 8, rows), jnp.float32),
                pltpu.VMEM((UNITS, HD, rows), jnp.float32),
                pltpu.VMEM((PAIRS, HEADS, 2 * BLK, rows), jnp.float32),
            ],
            compiler_params=params(12),
            cost_estimate=COST,
            name="attend" + "".join(map(str, steps)),
        )(lists, cached_lens, new_counts, *[x for i in steps for x in qs[i]], k, v)

    msg1, msg3 = attend(1, 3)
    (msg2,) = attend(2)
    (msg0,) = attend(0)
    joined = pl.pallas_call(
        join_kernel,
        out_shape=jax.ShapeDtypeStruct((MSG, 8 * BLK), jnp.float32),
        in_specs=[VMEM] * 2,
        out_specs=VMEM,
        compiler_params=params(12),
        cost_estimate=COST,
        name="join",
    )(turn(msg1, "y", 4, -1), turn(msg3, "y", 4, -3))
    msg = pl.pallas_call(
        fold_kernel,
        out_shape=jax.ShapeDtypeStruct((32, LAST, HD), jnp.bfloat16),
        in_specs=[VMEM] * 3,
        out_specs=VMEM,
        compiler_params=params(12),
        name="fold",
    )(joined, msg0, turn(msg2, "y", 4, -2))
    msg = lax.all_to_all(msg, ("z", "xh", "kvh"), split_axis=0, concat_axis=0, tiled=True)
    return pl.pallas_call(
        finish_kernel,
        out_shape=jax.ShapeDtypeStruct((1, 64, HD), jnp.bfloat16),
        in_specs=[VMEM],
        out_specs=VMEM,
        compiler_params=params(12),
        name="finish",
    )(msg)


def solution(mesh):
    split = Mesh(mesh.devices.reshape(8, 4, 2, 2, 2), ("z", "y", "xh", "core", "kvh"))
    ctx = ("z", "y", "xh", "core")
    in_specs = (
        P(ctx, "kvh", None, None),
        P(ctx, "kvh", None),
        P(ctx, "kvh", None),
        P(ctx),
        P(),
        P(),
    )
    return jax.shard_map(
        per_device,
        mesh=split,
        in_specs=in_specs,
        out_specs=P(ctx + ("kvh",), None, None),
        check_vma=False,
    )
```

```python
import functools

import jax
import jax.numpy as jnp
from jax import lax
from jax.experimental import pallas as pl
from jax.experimental.pallas import tpu as pltpu
from jax.sharding import Mesh, PartitionSpec as P

LOG2E = 1.4426950408889634
FLOOR = -1e29
MASKED = -1e30

BLK = 128
OWN = 12
BOTH = 2 * OWN
HEADS = 2
GROUP = 16
HD = 128
SEQS = 4
UNITS = SEQS * HEADS
MSG = HD + 8
BEYOND = 1 << 20
PAIRS = (BOTH + SEQS) // 2
WIDE = HEADS * BLK
LAST = HEADS * GROUP + 8
SMEM = pl.BlockSpec(memory_space=pltpu.SMEM)
VMEM = pl.BlockSpec(memory_space=pltpu.VMEM)
COST = pl.CostEstimate(flops=1_000_000_000, bytes_accessed=4 << 20, transcendentals=0)


def split3(x):
    hi = x.astype(jnp.bfloat16).astype(jnp.float32)
    rest = x - hi
    mid = rest.astype(jnp.bfloat16).astype(jnp.float32)
    return hi, mid, rest - mid


def select_kernel(own_ids, peer_ids, cached, counts, list_ref):
    blocks_per_seq = (BOTH * 64) // SEQS
    found = []
    for b in range(BOTH):
        ident = own_ids[b] if b < OWN else peer_ids[b - OWN]
        s = sum((ident >= n * blocks_per_seq).astype(jnp.int32) for n in range(1, SEQS))
        number = ident - s * blocks_per_seq
        found.append((s, number, number * BLK <= cached[s] + counts[s] - 1))
    at = []
    end = jnp.int32(0)
    for n in range(SEQS):
        at.append(end)
        here = sum(((s == n) & hit).astype(jnp.int32) for s, _, hit in found)
        end = end + ((here + 1) & -2)
    pairs = ((end >> 1) + 1) & -2
    for e in range(2 * PAIRS):
        list_ref[0, e] = 0
        list_ref[1, e] = BEYOND
    for p in range(PAIRS):
        list_ref[2, p] = sum((p >= (at[n] >> 1)).astype(jnp.int32) for n in range(1, SEQS))
    for n in range(SEQS):
        list_ref[2, 16 + n] = at[n]
    for b, (s, number, hit) in enumerate(found):
        e = jnp.where(hit, list_ref[2, 16 + s], 31)
        list_ref[0, e] = b
        list_ref[1, e] = number
        list_ref[2, 16 + s] += hit.astype(jnp.int32)
    list_ref[2, 31] = pairs


def pack_kernel(lists, k0, k1, v0, v1, k_ref, v_ref):
    def place_pair(p, _):
        for i in range(2):
            here = slice(i * BLK, (i + 1) * BLK)
            b = lists[0, 2 * p + i]

            def put(k_from, v_from, first):
                rows = pl.ds(pl.multiple_of((b - first) * BLK, BLK), BLK)
                for h in range(HEADS):
                    k_ref[p, h, here, :] = k_from[h, rows, :]
                    v_ref[p, h, :, here] = jnp.transpose(v_from[h, rows, :])

            pl.when(b < OWN)(lambda: put(k0, v0, 0))
            pl.when(b >= OWN)(lambda: put(k1, v1, OWN))
        return 0

    lax.fori_loop(0, lists[2, 31], place_pair, 0)


def attend_kernel(steps, *refs):
    n = len(steps)
    lists, cached, counts = refs[:3]
    q_refs, (k_ref, v_ref) = refs[3:3 + 2 * n], refs[3 + 2 * n:5 + 2 * n]
    out_refs, (m_ref, l_ref, acc_ref, t_ref) = refs[5 + 2 * n:5 + 3 * n], refs[5 + 3 * n:]
    rows = BLK * n
    lane = lax.broadcasted_iota(jnp.int32, (1, rows), 1)
    far = steps[0] if n == 1 else jnp.where(lane < BLK, steps[0], steps[1])
    within = (
        32 * ((lane >> 5) & 1)
        + 8 * ((lax.axis_index("y") + far) & 3)
        + 4 * (((lane >> 6) + lax.axis_index("xh")) & 1)
        + 2 * lax.axis_index("core")
        + ((lane >> 4) & 1)
    )
    slot = lax.broadcasted_iota(jnp.int32, (BLK, rows), 0)
    scale = LOG2E * HD ** -0.5
    count = lists[2, 31]
    m_ref[...] = jnp.full(m_ref.shape, FLOOR, jnp.float32)
    l_ref[...] = jnp.zeros(l_ref.shape, jnp.float32)
    acc_ref[...] = jnp.zeros(acc_ref.shape, jnp.float32)

    def score(j, _):
        for p in (2 * j, 2 * j + 1):
            s = lists[2, p]
            qpos = jnp.where(within < counts[s], cached[s] + within, -1)
            for h in range(HEADS):
                unit = s * HEADS + h
                q = jnp.concatenate(
                    [r[pl.ds(2 * s, 2), :, h].reshape(BLK // 2, HD) for r in q_refs], axis=0
                )
                t = lax.dot_general(
                    k_ref[p, h], q, (((1,), (1,)), ((), ())), preferred_element_type=jnp.float32
                )
                top = None
                for i in range(2):
                    limit = qpos - lists[1, 2 * p + i] * BLK
                    part = jnp.where(slot <= limit, t[i * BLK:(i + 1) * BLK] * scale, MASKED)
                    t_ref[p, h, i * BLK:(i + 1) * BLK, :] = part
                    peak = jnp.max(part.reshape(BLK // 8, 8, rows), axis=0)
                    top = peak if top is None else jnp.maximum(top, peak)
                m_ref[unit] = jnp.maximum(m_ref[unit], top)
        return 0

    lax.fori_loop(0, count >> 1, score, 0)
    for unit in range(UNITS):
        m_ref[unit] = jnp.broadcast_to(
            jnp.max(m_ref[unit], axis=0, keepdims=True), (8, rows)
        )

    def weigh(j, _):
        for p in (2 * j, 2 * j + 1):
            s = lists[2, p]
            for h in range(HEADS):
                unit = s * HEADS + h
                w = jnp.exp2(t_ref[p, h].reshape(2 * BLK // 8, 8, rows) - m_ref[unit][None])
                l_ref[unit] += jnp.sum(w, axis=0)
                acc_ref[unit] += jnp.dot(
                    v_ref[p, h],
                    w.reshape(2 * BLK, rows).astype(jnp.bfloat16),
                    preferred_element_type=jnp.float32,
                )
        return 0

    lax.fori_loop(0, count >> 1, weigh, 0)

    for unit in range(UNITS):
        total = jnp.sum(l_ref[unit], axis=0, keepdims=True)
        some = total > 0.0
        safe = jnp.where(some, total, 1.0)
        lse = jnp.where(some, m_ref[unit, 0:1, :] + jnp.log(safe) * LOG2E, MASKED)
        ctx = acc_ref[unit] * (1.0 / safe)
        tail = jnp.concatenate(split3(lse) + (jnp.zeros((5, rows), jnp.float32),), axis=0)
        for i, out_ref in enumerate(out_refs):
            cols = slice(i * BLK, (i + 1) * BLK)
            there = slice(unit * BLK, (unit + 1) * BLK)
            out_ref[0:HD, there] = ctx[:, cols].astype(jnp.bfloat16)
            out_ref[HD:MSG, there] = tail[:, cols].astype(jnp.bfloat16)


def logs_of(ref, there):
    t = ref[HD:MSG, there].astype(jnp.float32)
    return t[0:1] + t[1:2] + t[2:3]


def join_kernel(in0, in1, out_ref):
    for unit in range(UNITS):
        there = slice(unit * BLK, (unit + 1) * BLK)
        logs = [logs_of(r, there) for r in (in0, in1)]
        top = jnp.maximum(*logs)
        w = [jnp.exp2(x - top) for x in logs]
        out_ref[0:HD, there] = (
            in0[0:HD, there].astype(jnp.float32) * w[0]
            + in1[0:HD, there].astype(jnp.float32) * w[1]
        )
        out_ref[HD:MSG, there] = jnp.concatenate(
            [top, w[0] + w[1], jnp.zeros((6, BLK), jnp.float32)], axis=0
        )


def fold_kernel(joined, in0, in1, out_ref):
    def dest(s, e):
        return 8 * s + 4 * ((e >> 1) & 1) + 2 * ((lax.axis_index("xh") + (e >> 2)) & 1) + (e & 1)

    for s in range(SEQS):
        tails = []
        for h in range(HEADS):
            unit = s * HEADS + h
            there = slice(unit * BLK, (unit + 1) * BLK)
            logs = [joined[HD:HD + 1, there], logs_of(in0, there), logs_of(in1, there)]
            top = functools.reduce(jnp.maximum, logs)
            w = [jnp.exp2(x - top) for x in logs]
            total = joined[HD + 1:HD + 2, there] * w[0] + w[1] + w[2]
            inv = 1.0 / total
            ctx = (
                joined[0:HD, there] * (w[0] * inv)
                + in0[0:HD, there].astype(jnp.float32) * (w[1] * inv)
                + in1[0:HD, there].astype(jnp.float32) * (w[2] * inv)
            )
            ctx = jnp.transpose(ctx).astype(jnp.bfloat16)
            for e in range(8):
                out_ref[dest(s, e), h * GROUP:(h + 1) * GROUP, :] = ctx[e * GROUP:(e + 1) * GROUP]
            tails.extend(split3(top + jnp.log(total) * LOG2E))
        tail = jnp.concatenate(tails + [jnp.zeros((2, BLK), jnp.float32)], axis=0)
        for e in range(8):
            turned = tail if e == 0 else pltpu.roll(tail, BLK - GROUP * e, 1)
            out_ref[dest(s, e), 32:LAST, :] = turned.astype(jnp.bfloat16)


def finish_kernel(in_ref, out_ref):
    for kvh in range(2):
        sources = [2 * n + kvh for n in range(16)]
        t = jnp.concatenate(
            [in_ref[n, 32:LAST, :].astype(jnp.float32) for n in sources], axis=0
        )
        t = jnp.transpose(t)[0:GROUP]
        cols = t + pltpu.roll(t, BLK - 1, 1) + pltpu.roll(t, BLK - 2, 1)
        for h in range(HEADS):
            logs = []
            for n in range(16):
                at = n * 8 + 3 * h
                logs.append(jnp.broadcast_to(cols[:, at:at + 1], (GROUP, HD)))
            top = functools.reduce(jnp.maximum, logs)
            total = jnp.zeros((GROUP, HD), jnp.float32)
            ctx = jnp.zeros((GROUP, HD), jnp.float32)
            for n in range(16):
                w = jnp.exp2(logs[n] - top)
                total = total + w
                ctx = ctx + w * in_ref[
                    sources[n], h * GROUP:(h + 1) * GROUP, :
                ].astype(jnp.float32)
            first = kvh * 32 + h * GROUP
            out_ref[0, first:first + GROUP, :] = (ctx / total).astype(jnp.bfloat16)


def turn(x, axis, size, step):
    return lax.ppermute(x, axis, [((i + step) % size, i) for i in range(size)])


def params(mib):
    return pltpu.CompilerParams(vmem_limit_bytes=mib << 20)


def per_device(queries, k_cache, v_cache, block_owner, cached_lens, new_counts):
    k0, v0 = (x.reshape(OWN * WIDE, HD) for x in (k_cache, v_cache))
    k1, v1, ids = (turn(x, "core", 2, 1) for x in (k0, v0, block_owner))

    lists = pl.pallas_call(
        select_kernel,
        out_shape=jax.ShapeDtypeStruct((3, 32), jnp.int32),
        in_specs=[SMEM] * 4,
        out_specs=SMEM,
        compiler_params=params(12),
        name="select",
    )(block_owner, ids, cached_lens, new_counts)

    q = jnp.broadcast_to(queries[None], (8,) + queries.shape)
    q = lax.all_to_all(q, "z", split_axis=0, concat_axis=0, tiled=True)
    q, lists, *caches = lax.optimization_barrier((q, lists, k0, k1, v0, v1))
    k0, k1, v0, v1 = (
        jnp.transpose(x.reshape(OWN * BLK, HEADS, HD), (1, 0, 2)) for x in caches
    )
    k, v = pl.pallas_call(
        pack_kernel,
        out_shape=[
            jax.ShapeDtypeStruct((PAIRS, HEADS, 2 * BLK, HD), jnp.bfloat16),
            jax.ShapeDtypeStruct((PAIRS, HEADS, HD, 2 * BLK), jnp.bfloat16),
        ],
        in_specs=[SMEM] + [VMEM] * 4,
        out_specs=[VMEM, VMEM],
        compiler_params=params(12),
        cost_estimate=COST,
        name="pack",
    )(lists, k0, k1, v0, v1)
    over, near, back = lax.optimization_barrier(
        (turn(q, "xh", 2, 1), turn(q, "y", 4, 1), turn(q, "y", 4, 3))
    )
    near, back = [near, turn(over, "y", 4, 1)], [back, turn(over, "y", 4, 3)]
    back[1], k, v = lax.optimization_barrier((back[1], k, v))
    qs = [[q, over], near, [turn(near[0], "y", 4, 1), turn(back[1], "y", 4, 3)], back]

    def attend(*steps):
        n = len(steps)
        rows = n * BLK
        return pl.pallas_call(
            functools.partial(attend_kernel, steps),
            out_shape=[jax.ShapeDtypeStruct((MSG, 8 * BLK), jnp.bfloat16)] * n,
            in_specs=[SMEM] * 3 + [VMEM] * (2 * n + 2),
            out_specs=[VMEM] * n,
            scratch_shapes=[
                pltpu.VMEM((UNITS, 8, rows), jnp.float32),
                pltpu.VMEM((UNITS, 8, rows), jnp.float32),
                pltpu.VMEM((UNITS, HD, rows), jnp.float32),
                pltpu.VMEM((PAIRS, HEADS, 2 * BLK, rows), jnp.float32),
            ],
            compiler_params=params(12),
            cost_estimate=COST,
            name="attend" + "".join(map(str, steps)),
        )(lists, cached_lens, new_counts, *[x for i in steps for x in qs[i]], k, v)

    msg1, msg3 = attend(1, 3)
    (msg2,) = attend(2)
    (msg0,) = attend(0)
    msg2, msg3 = lax.optimization_barrier((msg2, msg3))
    joined = pl.pallas_call(
        join_kernel,
        out_shape=jax.ShapeDtypeStruct((MSG, 8 * BLK), jnp.float32),
        in_specs=[VMEM] * 2,
        out_specs=VMEM,
        compiler_params=params(12),
        cost_estimate=COST,
        name="join",
    )(msg0, turn(msg1, "y", 4, -1))
    msg = pl.pallas_call(
        fold_kernel,
        out_shape=jax.ShapeDtypeStruct((32, LAST, HD), jnp.bfloat16),
        in_specs=[VMEM] * 3,
        out_specs=VMEM,
        compiler_params=params(12),
        name="fold",
    )(joined, turn(msg2, "y", 4, -2), turn(msg3, "y", 4, -3))
    msg = lax.all_to_all(msg, ("z", "xh", "kvh"), split_axis=0, concat_axis=0, tiled=True)
    return pl.pallas_call(
        finish_kernel,
        out_shape=jax.ShapeDtypeStruct((1, 64, HD), jnp.bfloat16),
        in_specs=[VMEM],
        out_specs=VMEM,
        compiler_params=params(12),
        name="finish",
    )(msg)


def solution(mesh):
    split = Mesh(mesh.devices.reshape(8, 4, 2, 2, 2), ("z", "y", "xh", "core", "kvh"))
    ctx = ("z", "y", "xh", "core")
    in_specs = (
        P(ctx, "kvh", None, None),
        P(ctx, "kvh", None),
        P(ctx, "kvh", None),
        P(ctx),
        P(),
        P(),
    )
    return jax.shard_map(
        per_device,
        mesh=split,
        in_specs=in_specs,
        out_specs=P(ctx + ("kvh",), None, None),
        check_vma=False,
    )
```

```python
import functools

import jax
import jax.numpy as jnp
from jax import lax
from jax.experimental import pallas as pl
from jax.experimental.pallas import tpu as pltpu
from jax.sharding import Mesh, PartitionSpec as P

LOG2E = 1.4426950408889634
FLOOR = -1e29
MASKED = -1e30

BLK = 128
OWN = 12
BOTH = 2 * OWN
HEADS = 2
GROUP = 16
HD = 128
SEQS = 4
UNITS = SEQS * HEADS
MSG = HD + 8
BEYOND = 1 << 20
PAIRS = (BOTH + SEQS) // 2
WIDE = HEADS * BLK
LAST = HEADS * GROUP + 8
SMEM = pl.BlockSpec(memory_space=pltpu.SMEM)
VMEM = pl.BlockSpec(memory_space=pltpu.VMEM)
COST = pl.CostEstimate(flops=1_000_000_000, bytes_accessed=4 << 20, transcendentals=0)


def split3(x):
    hi = x.astype(jnp.bfloat16).astype(jnp.float32)
    rest = x - hi
    mid = rest.astype(jnp.bfloat16).astype(jnp.float32)
    return hi, mid, rest - mid


def select_kernel(meta, list_ref):
    blocks_per_seq = (BOTH * 64) // SEQS
    found = []
    for b in range(BOTH):
        ident = meta[b]
        s = sum((ident >= n * blocks_per_seq).astype(jnp.int32) for n in range(1, SEQS))
        number = ident - s * blocks_per_seq
        found.append((s, number, number * BLK <= meta[BOTH + s] + meta[BOTH + SEQS + s] - 1))
    at = []
    end = jnp.int32(0)
    for n in range(SEQS):
        at.append(end)
        here = sum(((s == n) & hit).astype(jnp.int32) for s, _, hit in found)
        end = end + ((here + 1) & -2)
    pairs = ((end >> 1) + 1) & -2
    for e in range(2 * PAIRS):
        list_ref[0, e] = 0
        list_ref[1, e] = BEYOND
    for p in range(PAIRS):
        list_ref[2, p] = sum((p >= (at[n] >> 1)).astype(jnp.int32) for n in range(1, SEQS))
    for n in range(SEQS):
        list_ref[2, 16 + n] = at[n]
    for b, (s, number, hit) in enumerate(found):
        e = jnp.where(hit, list_ref[2, 16 + s], 31)
        list_ref[0, e] = b
        list_ref[1, e] = number
        list_ref[2, 16 + s] += hit.astype(jnp.int32)
    list_ref[2, 31] = pairs


def pack_kernel(lists, k0, k1, v0, v1, k_ref, v_ref):
    def place_pair(p, _):
        for i in range(2):
            here = slice(i * BLK, (i + 1) * BLK)
            b = lists[0, 2 * p + i]

            def put(k_from, v_from, first):
                rows = pl.ds(pl.multiple_of((b - first) * BLK, BLK), BLK)
                for h in range(HEADS):
                    k_ref[p, h, here, :] = k_from[h, rows, :]
                    v_ref[p, h, :, here] = jnp.transpose(v_from[h, rows, :])

            pl.when(b < OWN)(lambda: put(k0, v0, 0))
            pl.when(b >= OWN)(lambda: put(k1, v1, OWN))
        return 0

    lax.fori_loop(0, lists[2, 31], place_pair, 0)


def attend_kernel(steps, *refs):
    n = len(steps)
    lists, cached, counts = refs[:3]
    q_refs, (k_ref, v_ref) = refs[3:3 + 2 * n], refs[3 + 2 * n:5 + 2 * n]
    out_refs, (m_ref, l_ref, acc_ref, t_ref) = refs[5 + 2 * n:5 + 3 * n], refs[5 + 3 * n:]
    rows = BLK * n
    lane = lax.broadcasted_iota(jnp.int32, (1, rows), 1)
    far = steps[0] if n == 1 else jnp.where(lane < BLK, steps[0], steps[1])
    within = (
        32 * ((lane >> 5) & 1)
        + 8 * ((lax.axis_index("y") + far) & 3)
        + 4 * (((lane >> 6) + lax.axis_index("xh")) & 1)
        + 2 * lax.axis_index("core")
        + ((lane >> 4) & 1)
    )
    slot = lax.broadcasted_iota(jnp.int32, (BLK, rows), 0)
    scale = LOG2E * HD ** -0.5
    count = lists[2, 31]
    m_ref[...] = jnp.full(m_ref.shape, FLOOR, jnp.float32)
    l_ref[...] = jnp.zeros(l_ref.shape, jnp.float32)
    acc_ref[...] = jnp.zeros(acc_ref.shape, jnp.float32)

    def score(j, _):
        for p in (2 * j, 2 * j + 1):
            s = lists[2, p]
            qpos = jnp.where(within < counts[s], cached[s] + within, -1)
            for h in range(HEADS):
                unit = s * HEADS + h
                q = jnp.concatenate(
                    [r[pl.ds(2 * s, 2), :, h].reshape(BLK // 2, HD) for r in q_refs], axis=0
                )
                t = lax.dot_general(
                    k_ref[p, h], q, (((1,), (1,)), ((), ())), preferred_element_type=jnp.float32
                )
                top = None
                for i in range(2):
                    limit = qpos - lists[1, 2 * p + i] * BLK
                    part = jnp.where(slot <= limit, t[i * BLK:(i + 1) * BLK] * scale, MASKED)
                    t_ref[p, h, i * BLK:(i + 1) * BLK, :] = part
                    peak = jnp.max(part.reshape(BLK // 8, 8, rows), axis=0)
                    top = peak if top is None else jnp.maximum(top, peak)
                m_ref[unit] = jnp.maximum(m_ref[unit], top)
        return 0

    lax.fori_loop(0, count >> 1, score, 0)
    for unit in range(UNITS):
        m_ref[unit] = jnp.broadcast_to(
            jnp.max(m_ref[unit], axis=0, keepdims=True), (8, rows)
        )

    def weigh(j, _):
        for p in (2 * j, 2 * j + 1):
            s = lists[2, p]
            for h in range(HEADS):
                unit = s * HEADS + h
                w = jnp.exp2(t_ref[p, h].reshape(2 * BLK // 8, 8, rows) - m_ref[unit][None])
                l_ref[unit] += jnp.sum(w, axis=0)
                acc_ref[unit] += jnp.dot(
                    v_ref[p, h],
                    w.reshape(2 * BLK, rows).astype(jnp.bfloat16),
                    preferred_element_type=jnp.float32,
                )
        return 0

    lax.fori_loop(0, count >> 1, weigh, 0)

    for unit in range(UNITS):
        total = jnp.sum(l_ref[unit], axis=0, keepdims=True)
        some = total > 0.0
        safe = jnp.where(some, total, 1.0)
        lse = jnp.where(some, m_ref[unit, 0:1, :] + jnp.log(safe) * LOG2E, MASKED)
        ctx = acc_ref[unit] * (1.0 / safe)
        tail = jnp.concatenate(split3(lse) + (jnp.zeros((5, rows), jnp.float32),), axis=0)
        for i, out_ref in enumerate(out_refs):
            cols = slice(i * BLK, (i + 1) * BLK)
            there = slice(unit * BLK, (unit + 1) * BLK)
            out_ref[0:HD, there] = ctx[:, cols].astype(jnp.bfloat16)
            out_ref[HD:MSG, there] = tail[:, cols].astype(jnp.bfloat16)


def logs_of(ref, there):
    t = ref[HD:MSG, there].astype(jnp.float32)
    return t[0:1] + t[1:2] + t[2:3]


def join_kernel(in0, in1, out_ref):
    for unit in range(UNITS):
        there = slice(unit * BLK, (unit + 1) * BLK)
        logs = [logs_of(r, there) for r in (in0, in1)]
        top = jnp.maximum(*logs)
        w = [jnp.exp2(x - top) for x in logs]
        out_ref[0:HD, there] = (
            in0[0:HD, there].astype(jnp.float32) * w[0]
            + in1[0:HD, there].astype(jnp.float32) * w[1]
        )
        out_ref[HD:MSG, there] = jnp.concatenate(
            [top, w[0] + w[1], jnp.zeros((6, BLK), jnp.float32)], axis=0
        )


def fold_kernel(joined, in0, in1, out_ref):
    def dest(s, e):
        return 8 * s + 4 * ((e >> 1) & 1) + 2 * ((lax.axis_index("xh") + (e >> 2)) & 1) + (e & 1)

    for s in range(SEQS):
        tails = []
        for h in range(HEADS):
            unit = s * HEADS + h
            there = slice(unit * BLK, (unit + 1) * BLK)
            logs = [joined[HD:HD + 1, there], logs_of(in0, there), logs_of(in1, there)]
            top = functools.reduce(jnp.maximum, logs)
            w = [jnp.exp2(x - top) for x in logs]
            total = joined[HD + 1:HD + 2, there] * w[0] + w[1] + w[2]
            inv = 1.0 / total
            ctx = (
                joined[0:HD, there] * (w[0] * inv)
                + in0[0:HD, there].astype(jnp.float32) * (w[1] * inv)
                + in1[0:HD, there].astype(jnp.float32) * (w[2] * inv)
            )
            ctx = jnp.transpose(ctx).astype(jnp.bfloat16)
            for e in range(8):
                out_ref[dest(s, e), h * GROUP:(h + 1) * GROUP, :] = ctx[e * GROUP:(e + 1) * GROUP]
            tails.extend(split3(top + jnp.log(total) * LOG2E))
        tail = jnp.concatenate(tails + [jnp.zeros((2, BLK), jnp.float32)], axis=0)
        for e in range(8):
            turned = tail if e == 0 else pltpu.roll(tail, BLK - GROUP * e, 1)
            out_ref[dest(s, e), 32:LAST, :] = turned.astype(jnp.bfloat16)


def finish_kernel(in_ref, out_ref):
    for kvh in range(2):
        sources = [2 * n + kvh for n in range(16)]
        t = jnp.concatenate(
            [in_ref[n, 32:LAST, :].astype(jnp.float32) for n in sources], axis=0
        )
        t = jnp.transpose(t)[0:GROUP]
        cols = t + pltpu.roll(t, BLK - 1, 1) + pltpu.roll(t, BLK - 2, 1)
        for h in range(HEADS):
            logs = []
            for n in range(16):
                at = n * 8 + 3 * h
                logs.append(jnp.broadcast_to(cols[:, at:at + 1], (GROUP, HD)))
            top = functools.reduce(jnp.maximum, logs)
            total = jnp.zeros((GROUP, HD), jnp.float32)
            ctx = jnp.zeros((GROUP, HD), jnp.float32)
            for n in range(16):
                w = jnp.exp2(logs[n] - top)
                total = total + w
                ctx = ctx + w * in_ref[
                    sources[n], h * GROUP:(h + 1) * GROUP, :
                ].astype(jnp.float32)
            first = kvh * 32 + h * GROUP
            out_ref[0, first:first + GROUP, :] = (ctx / total).astype(jnp.bfloat16)


def turn(x, axis, size, step):
    return lax.ppermute(x, axis, [((i + step) % size, i) for i in range(size)])


def params(mib):
    return pltpu.CompilerParams(vmem_limit_bytes=mib << 20)


def by_head(x):
    return jnp.transpose(x.reshape(OWN * BLK, HEADS, HD), (1, 0, 2))


def per_device(queries, k_cache, v_cache, block_owner, cached_lens, new_counts):
    k0, v0 = (x.reshape(OWN * WIDE, HD) for x in (k_cache, v_cache))
    k1, v1, ids = (turn(x, "core", 2, 1) for x in (k0, v0, block_owner))

    lists = pl.pallas_call(
        select_kernel,
        out_shape=jax.ShapeDtypeStruct((3, 32), jnp.int32),
        in_specs=[SMEM],
        out_specs=SMEM,
        compiler_params=params(12),
        name="select",
    )(jnp.concatenate([block_owner, ids, cached_lens, new_counts]))

    q = jnp.broadcast_to(queries[None], (8,) + queries.shape)
    q = lax.all_to_all(q, "z", split_axis=0, concat_axis=0, tiled=True)
    k0, v0 = by_head(k0), by_head(v0)
    q, lists, k0, k1, v0, v1 = lax.optimization_barrier((q, lists, k0, k1, v0, v1))
    k1, v1 = by_head(k1), by_head(v1)
    k, v = pl.pallas_call(
        pack_kernel,
        out_shape=[
            jax.ShapeDtypeStruct((PAIRS, HEADS, 2 * BLK, HD), jnp.bfloat16),
            jax.ShapeDtypeStruct((PAIRS, HEADS, HD, 2 * BLK), jnp.bfloat16),
        ],
        in_specs=[SMEM] + [VMEM] * 4,
        out_specs=[VMEM, VMEM],
        compiler_params=params(12),
        cost_estimate=COST,
        name="pack",
    )(lists, k0, k1, v0, v1)
    over, near, back, k, v = lax.optimization_barrier(
        (turn(q, "xh", 2, 1), turn(q, "y", 4, 1), turn(q, "y", 4, 3), k, v)
    )
    near, back = [near, turn(over, "y", 4, 1)], [back, turn(over, "y", 4, 3)]
    qs = [[q, over], near, [turn(near[0], "y", 4, 1), turn(back[1], "y", 4, 3)], back]

    def attend(*steps):
        n = len(steps)
        rows = n * BLK
        return pl.pallas_call(
            functools.partial(attend_kernel, steps),
            out_shape=[jax.ShapeDtypeStruct((MSG, 8 * BLK), jnp.bfloat16)] * n,
            in_specs=[SMEM] * 3 + [VMEM] * (2 * n + 2),
            out_specs=[VMEM] * n,
            scratch_shapes=[
                pltpu.VMEM((UNITS, 8, rows), jnp.float32),
                pltpu.VMEM((UNITS, 8, rows), jnp.float32),
                pltpu.VMEM((UNITS, HD, rows), jnp.float32),
                pltpu.VMEM((PAIRS, HEADS, 2 * BLK, rows), jnp.float32),
            ],
            compiler_params=params(12),
            cost_estimate=COST,
            name="attend" + "".join(map(str, steps)),
        )(lists, cached_lens, new_counts, *[x for i in steps for x in qs[i]], k, v)

    msg1, msg3 = attend(1, 3)
    (msg2,) = attend(2)
    (msg0,) = attend(0)
    joined = pl.pallas_call(
        join_kernel,
        out_shape=jax.ShapeDtypeStruct((MSG, 8 * BLK), jnp.float32),
        in_specs=[VMEM] * 2,
        out_specs=VMEM,
        compiler_params=params(12),
        cost_estimate=COST,
        name="join",
    )(turn(msg1, "y", 4, -1), turn(msg3, "y", 4, -3))
    msg = pl.pallas_call(
        fold_kernel,
        out_shape=jax.ShapeDtypeStruct((32, LAST, HD), jnp.bfloat16),
        in_specs=[VMEM] * 3,
        out_specs=VMEM,
        compiler_params=params(12),
        name="fold",
    )(joined, msg0, turn(msg2, "y", 4, -2))
    msg = lax.all_to_all(msg, ("z", "xh", "kvh"), split_axis=0, concat_axis=0, tiled=True)
    return pl.pallas_call(
        finish_kernel,
        out_shape=jax.ShapeDtypeStruct((1, 64, HD), jnp.bfloat16),
        in_specs=[VMEM],
        out_specs=VMEM,
        compiler_params=params(12),
        name="finish",
    )(msg)


def solution(mesh):
    split = Mesh(mesh.devices.reshape(8, 4, 2, 2, 2), ("z", "y", "xh", "core", "kvh"))
    ctx = ("z", "y", "xh", "core")
    in_specs = (
        P(ctx, "kvh", None, None),
        P(ctx, "kvh", None),
        P(ctx, "kvh", None),
        P(ctx),
        P(),
        P(),
    )
    return jax.shard_map(
        per_device,
        mesh=split,
        in_specs=in_specs,
        out_specs=P(ctx + ("kvh",), None, None),
        check_vma=False,
    )
```

```python
import functools

import jax
import jax.numpy as jnp
from jax import lax
from jax.experimental import pallas as pl
from jax.experimental.pallas import tpu as pltpu
from jax.sharding import Mesh, PartitionSpec as P

LOG2E = 1.4426950408889634
FLOOR = -1e29
MASKED = -1e30

BLK = 128
OWN = 12
BOTH = 2 * OWN
HEADS = 2
GROUP = 16
HD = 128
SEQS = 4
UNITS = SEQS * HEADS
MSG = HD + 8
BEYOND = 1 << 20
PAIRS = (BOTH + SEQS) // 2
WIDE = HEADS * BLK
LAST = HEADS * GROUP + 8
SMEM = pl.BlockSpec(memory_space=pltpu.SMEM)
VMEM = pl.BlockSpec(memory_space=pltpu.VMEM)
COST = pl.CostEstimate(flops=1_000_000_000, bytes_accessed=4 << 20, transcendentals=0)


def split3(x):
    hi = x.astype(jnp.bfloat16).astype(jnp.float32)
    rest = x - hi
    mid = rest.astype(jnp.bfloat16).astype(jnp.float32)
    return hi, mid, rest - mid


def select_kernel(meta, list_ref):
    blocks_per_seq = (BOTH * 64) // SEQS
    found = []
    for b in range(BOTH):
        ident = meta[b]
        s = sum((ident >= n * blocks_per_seq).astype(jnp.int32) for n in range(1, SEQS))
        number = ident - s * blocks_per_seq
        found.append((s, number, number * BLK <= meta[BOTH + s] + meta[BOTH + SEQS + s] - 1))
    at = []
    end = jnp.int32(0)
    for n in range(SEQS):
        at.append(end)
        here = sum(((s == n) & hit).astype(jnp.int32) for s, _, hit in found)
        end = end + ((here + 1) & -2)
    pairs = ((end >> 1) + 1) & -2
    for e in range(2 * PAIRS):
        list_ref[0, e] = 0
        list_ref[1, e] = BEYOND
    for p in range(PAIRS):
        list_ref[2, p] = sum((p >= (at[n] >> 1)).astype(jnp.int32) for n in range(1, SEQS))
    for n in range(SEQS):
        list_ref[2, 16 + n] = at[n]
    for b, (s, number, hit) in enumerate(found):
        e = jnp.where(hit, list_ref[2, 16 + s], 31)
        list_ref[0, e] = b
        list_ref[1, e] = number
        list_ref[2, 16 + s] += hit.astype(jnp.int32)
    list_ref[2, 31] = pairs


def pack_kernel(lists, k0, k1, v0, v1, k_ref, v_ref):
    def place_pair(p, _):
        for i in range(2):
            here = slice(i * BLK, (i + 1) * BLK)
            b = lists[0, 2 * p + i]

            def put(k_from, v_from, first):
                rows = pl.ds(pl.multiple_of((b - first) * BLK, BLK), BLK)
                for h in range(HEADS):
                    k_ref[p, h, here, :] = k_from[h, rows, :]
                    v_ref[p, h, :, here] = jnp.transpose(v_from[h, rows, :])

            pl.when(b < OWN)(lambda: put(k0, v0, 0))
            pl.when(b >= OWN)(lambda: put(k1, v1, OWN))
        return 0

    lax.fori_loop(0, lists[2, 31], place_pair, 0)


def attend_kernel(steps, *refs):
    n = len(steps)
    lists, cached, counts = refs[:3]
    q_refs, (k_ref, v_ref) = refs[3:3 + 2 * n], refs[3 + 2 * n:5 + 2 * n]
    out_refs, (m_ref, l_ref, acc_ref, t_ref) = refs[5 + 2 * n:5 + 3 * n], refs[5 + 3 * n:]
    rows = BLK * n
    lane = lax.broadcasted_iota(jnp.int32, (1, rows), 1)
    far = steps[0] if n == 1 else jnp.where(lane < BLK, steps[0], steps[1])
    within = (
        32 * ((lane >> 5) & 1)
        + 8 * ((lax.axis_index("y") + far) & 3)
        + 4 * (((lane >> 6) + lax.axis_index("xh")) & 1)
        + 2 * lax.axis_index("core")
        + ((lane >> 4) & 1)
    )
    slot = lax.broadcasted_iota(jnp.int32, (BLK, rows), 0)
    scale = LOG2E * HD ** -0.5
    count = lists[2, 31]
    m_ref[...] = jnp.full(m_ref.shape, FLOOR, jnp.float32)
    l_ref[...] = jnp.zeros(l_ref.shape, jnp.float32)
    acc_ref[...] = jnp.zeros(acc_ref.shape, jnp.float32)

    def score(j, _):
        for p in (2 * j, 2 * j + 1):
            s = lists[2, p]
            qpos = jnp.where(within < counts[s], cached[s] + within, -1)
            for h in range(HEADS):
                unit = s * HEADS + h
                q = jnp.concatenate(
                    [r[pl.ds(2 * s, 2), :, h].reshape(BLK // 2, HD) for r in q_refs], axis=0
                )
                t = lax.dot_general(
                    k_ref[p, h], q, (((1,), (1,)), ((), ())), preferred_element_type=jnp.float32
                )
                top = None
                for i in range(2):
                    limit = qpos - lists[1, 2 * p + i] * BLK
                    part = jnp.where(slot <= limit, t[i * BLK:(i + 1) * BLK] * scale, MASKED)
                    t_ref[p, h, i * BLK:(i + 1) * BLK, :] = part
                    peak = jnp.max(part.reshape(BLK // 8, 8, rows), axis=0)
                    top = peak if top is None else jnp.maximum(top, peak)
                m_ref[unit] = jnp.maximum(m_ref[unit], top)
        return 0

    lax.fori_loop(0, count >> 1, score, 0)
    for unit in range(UNITS):
        m_ref[unit] = jnp.broadcast_to(
            jnp.max(m_ref[unit], axis=0, keepdims=True), (8, rows)
        )

    def weigh(j, _):
        for p in (2 * j, 2 * j + 1):
            s = lists[2, p]
            for h in range(HEADS):
                unit = s * HEADS + h
                w = jnp.exp2(t_ref[p, h].reshape(2 * BLK // 8, 8, rows) - m_ref[unit][None])
                l_ref[unit] += jnp.sum(w, axis=0)
                acc_ref[unit] += jnp.dot(
                    v_ref[p, h],
                    w.reshape(2 * BLK, rows).astype(jnp.bfloat16),
                    preferred_element_type=jnp.float32,
                )
        return 0

    lax.fori_loop(0, count >> 1, weigh, 0)

    for unit in range(UNITS):
        total = jnp.sum(l_ref[unit], axis=0, keepdims=True)
        some = total > 0.0
        safe = jnp.where(some, total, 1.0)
        lse = jnp.where(some, m_ref[unit, 0:1, :] + jnp.log(safe) * LOG2E, MASKED)
        ctx = acc_ref[unit] * (1.0 / safe)
        tail = jnp.concatenate(split3(lse) + (jnp.zeros((5, rows), jnp.float32),), axis=0)
        for i, out_ref in enumerate(out_refs):
            cols = slice(i * BLK, (i + 1) * BLK)
            there = slice(unit * BLK, (unit + 1) * BLK)
            out_ref[0:HD, there] = ctx[:, cols].astype(jnp.bfloat16)
            out_ref[HD:MSG, there] = tail[:, cols].astype(jnp.bfloat16)


def logs_of(ref, there):
    t = ref[HD:MSG, there].astype(jnp.float32)
    return t[0:1] + t[1:2] + t[2:3]


def join_kernel(in0, in1, out_ref):
    for unit in range(UNITS):
        there = slice(unit * BLK, (unit + 1) * BLK)
        logs = [logs_of(r, there) for r in (in0, in1)]
        top = jnp.maximum(*logs)
        w = [jnp.exp2(x - top) for x in logs]
        out_ref[0:HD, there] = (
            in0[0:HD, there].astype(jnp.float32) * w[0]
            + in1[0:HD, there].astype(jnp.float32) * w[1]
        )
        out_ref[HD:MSG, there] = jnp.concatenate(
            [top, w[0] + w[1], jnp.zeros((6, BLK), jnp.float32)], axis=0
        )


def fold_kernel(joined, in0, in1, out_ref):
    def dest(s, e):
        return 8 * s + 4 * ((e >> 1) & 1) + 2 * ((lax.axis_index("xh") + (e >> 2)) & 1) + (e & 1)

    for s in range(SEQS):
        tails = []
        for h in range(HEADS):
            unit = s * HEADS + h
            there = slice(unit * BLK, (unit + 1) * BLK)
            logs = [joined[HD:HD + 1, there], logs_of(in0, there), logs_of(in1, there)]
            top = functools.reduce(jnp.maximum, logs)
            w = [jnp.exp2(x - top) for x in logs]
            total = joined[HD + 1:HD + 2, there] * w[0] + w[1] + w[2]
            inv = 1.0 / total
            ctx = (
                joined[0:HD, there] * (w[0] * inv)
                + in0[0:HD, there].astype(jnp.float32) * (w[1] * inv)
                + in1[0:HD, there].astype(jnp.float32) * (w[2] * inv)
            )
            ctx = jnp.transpose(ctx).astype(jnp.bfloat16)
            for e in range(8):
                out_ref[dest(s, e), h * GROUP:(h + 1) * GROUP, :] = ctx[e * GROUP:(e + 1) * GROUP]
            tails.extend(split3(top + jnp.log(total) * LOG2E))
        tail = jnp.concatenate(tails + [jnp.zeros((2, BLK), jnp.float32)], axis=0)
        for e in range(8):
            turned = tail if e == 0 else pltpu.roll(tail, BLK - GROUP * e, 1)
            out_ref[dest(s, e), 32:LAST, :] = turned.astype(jnp.bfloat16)


def finish_kernel(in_ref, out_ref):
    for kvh in range(2):
        sources = [2 * n + kvh for n in range(16)]
        t = jnp.concatenate(
            [in_ref[n, 32:LAST, :].astype(jnp.float32) for n in sources], axis=0
        )
        t = jnp.transpose(t)[0:GROUP]
        cols = t + pltpu.roll(t, BLK - 1, 1) + pltpu.roll(t, BLK - 2, 1)
        for h in range(HEADS):
            logs = []
            for n in range(16):
                at = n * 8 + 3 * h
                logs.append(jnp.broadcast_to(cols[:, at:at + 1], (GROUP, HD)))
            top = functools.reduce(jnp.maximum, logs)
            total = jnp.zeros((GROUP, HD), jnp.float32)
            ctx = jnp.zeros((GROUP, HD), jnp.float32)
            for n in range(16):
                w = jnp.exp2(logs[n] - top)
                total = total + w
                ctx = ctx + w * in_ref[
                    sources[n], h * GROUP:(h + 1) * GROUP, :
                ].astype(jnp.float32)
            first = kvh * 32 + h * GROUP
            out_ref[0, first:first + GROUP, :] = (ctx / total).astype(jnp.bfloat16)


def turn(x, axis, size, step):
    return lax.ppermute(x, axis, [((i + step) % size, i) for i in range(size)])


def params(mib):
    return pltpu.CompilerParams(vmem_limit_bytes=mib << 20)


def by_head(x):
    return jnp.transpose(x.reshape(OWN * BLK, HEADS, HD), (1, 0, 2))


def per_device(queries, k_cache, v_cache, block_owner, cached_lens, new_counts):
    k0, v0 = (x.reshape(OWN * WIDE, HD) for x in (k_cache, v_cache))
    k1, v1, ids = (turn(x, "core", 2, 1) for x in (k0, v0, block_owner))

    lists = pl.pallas_call(
        select_kernel,
        out_shape=jax.ShapeDtypeStruct((3, 32), jnp.int32),
        in_specs=[SMEM],
        out_specs=SMEM,
        compiler_params=params(12),
        name="select",
    )(jnp.concatenate([block_owner, ids, cached_lens, new_counts]))

    q = jnp.broadcast_to(queries[None], (8,) + queries.shape)
    q = lax.all_to_all(q, "z", split_axis=0, concat_axis=0, tiled=True)
    k0, v0 = by_head(k0), by_head(v0)
    q, lists, k0, k1, v0, v1 = lax.optimization_barrier((q, lists, k0, k1, v0, v1))
    k1, v1 = by_head(k1), by_head(v1)
    k, v = pl.pallas_call(
        pack_kernel,
        out_shape=[
            jax.ShapeDtypeStruct((PAIRS, HEADS, 2 * BLK, HD), jnp.bfloat16),
            jax.ShapeDtypeStruct((PAIRS, HEADS, HD, 2 * BLK), jnp.bfloat16),
        ],
        in_specs=[SMEM] + [VMEM] * 4,
        out_specs=[VMEM, VMEM],
        compiler_params=params(12),
        cost_estimate=COST,
        name="pack",
    )(lists, k0, k1, v0, v1)
    over, k, v = lax.optimization_barrier((turn(q, "xh", 2, 1), k, v))
    near, back = lax.optimization_barrier((turn(q, "y", 4, 1), turn(q, "y", 4, 3)))
    near, back = [near, turn(over, "y", 4, 1)], [back, turn(over, "y", 4, 3)]
    qs = [[q, over], near, [turn(near[0], "y", 4, 1), turn(back[1], "y", 4, 3)], back]

    def attend(*steps):
        n = len(steps)
        rows = n * BLK
        return pl.pallas_call(
            functools.partial(attend_kernel, steps),
            out_shape=[jax.ShapeDtypeStruct((MSG, 8 * BLK), jnp.bfloat16)] * n,
            in_specs=[SMEM] * 3 + [VMEM] * (2 * n + 2),
            out_specs=[VMEM] * n,
            scratch_shapes=[
                pltpu.VMEM((UNITS, 8, rows), jnp.float32),
                pltpu.VMEM((UNITS, 8, rows), jnp.float32),
                pltpu.VMEM((UNITS, HD, rows), jnp.float32),
                pltpu.VMEM((PAIRS, HEADS, 2 * BLK, rows), jnp.float32),
            ],
            compiler_params=params(12),
            cost_estimate=COST,
            name="attend" + "".join(map(str, steps)),
        )(lists, cached_lens, new_counts, *[x for i in steps for x in qs[i]], k, v)

    msg1, msg3 = attend(1, 3)
    (msg2,) = attend(2)
    (msg0,) = attend(0)
    joined = pl.pallas_call(
        join_kernel,
        out_shape=jax.ShapeDtypeStruct((MSG, 8 * BLK), jnp.float32),
        in_specs=[VMEM] * 2,
        out_specs=VMEM,
        compiler_params=params(12),
        cost_estimate=COST,
        name="join",
    )(turn(msg1, "y", 4, -1), turn(msg3, "y", 4, -3))
    msg = pl.pallas_call(
        fold_kernel,
        out_shape=jax.ShapeDtypeStruct((32, LAST, HD), jnp.bfloat16),
        in_specs=[VMEM] * 3,
        out_specs=VMEM,
        compiler_params=params(12),
        name="fold",
    )(joined, msg0, turn(msg2, "y", 4, -2))
    msg = lax.all_to_all(msg, ("z", "xh", "kvh"), split_axis=0, concat_axis=0, tiled=True)
    return pl.pallas_call(
        finish_kernel,
        out_shape=jax.ShapeDtypeStruct((1, 64, HD), jnp.bfloat16),
        in_specs=[VMEM],
        out_specs=VMEM,
        compiler_params=params(12),
        name="finish",
    )(msg)


def solution(mesh):
    split = Mesh(mesh.devices.reshape(8, 4, 2, 2, 2), ("z", "y", "xh", "core", "kvh"))
    ctx = ("z", "y", "xh", "core")
    in_specs = (
        P(ctx, "kvh", None, None),
        P(ctx, "kvh", None),
        P(ctx, "kvh", None),
        P(ctx),
        P(),
        P(),
    )
    return jax.shard_map(
        per_device,
        mesh=split,
        in_specs=in_specs,
        out_specs=P(ctx + ("kvh",), None, None),
        check_vma=False,
    )
```

```python
import functools

import jax
import jax.numpy as jnp
from jax import lax
from jax.experimental import pallas as pl
from jax.experimental.pallas import tpu as pltpu
from jax.sharding import Mesh, PartitionSpec as P

LOG2E = 1.4426950408889634
FLOOR = -1e29
MASKED = -1e30

BLK = 128
OWN = 12
BOTH = 2 * OWN
HEADS = 2
GROUP = 16
HD = 128
SEQS = 4
UNITS = SEQS * HEADS
MSG = HD + 8
BEYOND = 1 << 20
PAIRS = (BOTH + SEQS) // 2
WIDE = HEADS * BLK
LAST = HEADS * GROUP + 8
SMEM = pl.BlockSpec(memory_space=pltpu.SMEM)
VMEM = pl.BlockSpec(memory_space=pltpu.VMEM)
COST = pl.CostEstimate(flops=1_000_000_000, bytes_accessed=4 << 20, transcendentals=0)


def split3(x):
    hi = x.astype(jnp.bfloat16).astype(jnp.float32)
    rest = x - hi
    mid = rest.astype(jnp.bfloat16).astype(jnp.float32)
    return hi, mid, rest - mid


def select_kernel(meta, list_ref):
    blocks_per_seq = (BOTH * 64) // SEQS
    found = []
    for b in range(BOTH):
        ident = meta[b]
        s = sum((ident >= n * blocks_per_seq).astype(jnp.int32) for n in range(1, SEQS))
        number = ident - s * blocks_per_seq
        found.append((s, number, number * BLK <= meta[BOTH + s] + meta[BOTH + SEQS + s] - 1))
    at = []
    end = jnp.int32(0)
    for n in range(SEQS):
        at.append(end)
        here = sum(((s == n) & hit).astype(jnp.int32) for s, _, hit in found)
        end = end + ((here + 1) & -2)
    pairs = ((end >> 1) + 1) & -2
    for e in range(2 * PAIRS):
        list_ref[0, e] = 0
        list_ref[1, e] = BEYOND
    for p in range(PAIRS):
        list_ref[2, p] = sum((p >= (at[n] >> 1)).astype(jnp.int32) for n in range(1, SEQS))
    for n in range(SEQS):
        list_ref[2, 16 + n] = at[n]
    for b, (s, number, hit) in enumerate(found):
        e = jnp.where(hit, list_ref[2, 16 + s], 31)
        list_ref[0, e] = b
        list_ref[1, e] = number
        list_ref[2, 16 + s] += hit.astype(jnp.int32)
    list_ref[2, 31] = pairs


def pack_kernel(lists, k0, k1, v0, v1, k_ref, v_ref):
    def place_pair(p, _):
        for i in range(2):
            here = slice(i * BLK, (i + 1) * BLK)
            b = lists[0, 2 * p + i]

            def put(k_from, v_from, first):
                rows = pl.ds(pl.multiple_of((b - first) * BLK, BLK), BLK)
                for h in range(HEADS):
                    k_ref[p, h, here, :] = k_from[h, rows, :]
                    v_ref[p, h, :, here] = jnp.transpose(v_from[h, rows, :])

            pl.when(b < OWN)(lambda: put(k0, v0, 0))
            pl.when(b >= OWN)(lambda: put(k1, v1, OWN))
        return 0

    lax.fori_loop(0, lists[2, 31], place_pair, 0)


def attend_kernel(steps, *refs):
    n = len(steps)
    lists, cached, counts = refs[:3]
    q_refs, (k_ref, v_ref) = refs[3:3 + 2 * n], refs[3 + 2 * n:5 + 2 * n]
    out_refs, (m_ref, l_ref, acc_ref, t_ref) = refs[5 + 2 * n:5 + 3 * n], refs[5 + 3 * n:]
    rows = BLK * n
    lane = lax.broadcasted_iota(jnp.int32, (1, rows), 1)
    far = steps[0] if n == 1 else jnp.where(lane < BLK, steps[0], steps[1])
    within = (
        32 * ((lane >> 5) & 1)
        + 8 * ((lax.axis_index("y") + far) & 3)
        + 4 * (((lane >> 6) + lax.axis_index("xh")) & 1)
        + 2 * lax.axis_index("core")
        + ((lane >> 4) & 1)
    )
    slot = lax.broadcasted_iota(jnp.int32, (BLK, rows), 0)
    scale = LOG2E * HD ** -0.5
    count = lists[2, 31]
    m_ref[...] = jnp.full(m_ref.shape, FLOOR, jnp.float32)
    l_ref[...] = jnp.zeros(l_ref.shape, jnp.float32)
    acc_ref[...] = jnp.zeros(acc_ref.shape, jnp.float32)

    def score(j, _):
        for p in (2 * j, 2 * j + 1):
            s = lists[2, p]
            qpos = jnp.where(within < counts[s], cached[s] + within, -1)
            for h in range(HEADS):
                unit = s * HEADS + h
                q = jnp.concatenate(
                    [r[pl.ds(2 * s, 2), :, h].reshape(BLK // 2, HD) for r in q_refs], axis=0
                )
                t = lax.dot_general(
                    k_ref[p, h], q, (((1,), (1,)), ((), ())), preferred_element_type=jnp.float32
                )
                top = None
                for i in range(2):
                    limit = qpos - lists[1, 2 * p + i] * BLK
                    part = jnp.where(slot <= limit, t[i * BLK:(i + 1) * BLK] * scale, MASKED)
                    t_ref[p, h, i * BLK:(i + 1) * BLK, :] = part
                    peak = jnp.max(part.reshape(BLK // 8, 8, rows), axis=0)
                    top = peak if top is None else jnp.maximum(top, peak)
                m_ref[unit] = jnp.maximum(m_ref[unit], top)
        return 0

    lax.fori_loop(0, count >> 1, score, 0)
    for unit in range(UNITS):
        m_ref[unit] = jnp.broadcast_to(
            jnp.max(m_ref[unit], axis=0, keepdims=True), (8, rows)
        )

    def weigh(j, _):
        for p in (2 * j, 2 * j + 1):
            s = lists[2, p]
            for h in range(HEADS):
                unit = s * HEADS + h
                w = jnp.exp2(t_ref[p, h].reshape(2 * BLK // 8, 8, rows) - m_ref[unit][None])
                l_ref[unit] += jnp.sum(w, axis=0)
                acc_ref[unit] += jnp.dot(
                    v_ref[p, h],
                    w.reshape(2 * BLK, rows).astype(jnp.bfloat16),
                    preferred_element_type=jnp.float32,
                )
        return 0

    lax.fori_loop(0, count >> 1, weigh, 0)

    for unit in range(UNITS):
        total = jnp.sum(l_ref[unit], axis=0, keepdims=True)
        some = total > 0.0
        safe = jnp.where(some, total, 1.0)
        lse = jnp.where(some, m_ref[unit, 0:1, :] + jnp.log(safe) * LOG2E, MASKED)
        ctx = acc_ref[unit] * (1.0 / safe)
        tail = jnp.concatenate(split3(lse) + (jnp.zeros((5, rows), jnp.float32),), axis=0)
        for i, out_ref in enumerate(out_refs):
            cols = slice(i * BLK, (i + 1) * BLK)
            there = slice(unit * BLK, (unit + 1) * BLK)
            out_ref[0:HD, there] = ctx[:, cols].astype(jnp.bfloat16)
            out_ref[HD:MSG, there] = tail[:, cols].astype(jnp.bfloat16)


def logs_of(ref, there):
    t = ref[HD:MSG, there].astype(jnp.float32)
    return t[0:1] + t[1:2] + t[2:3]


def join_kernel(in0, in1, out_ref):
    for unit in range(UNITS):
        there = slice(unit * BLK, (unit + 1) * BLK)
        logs = [logs_of(r, there) for r in (in0, in1)]
        top = jnp.maximum(*logs)
        w = [jnp.exp2(x - top) for x in logs]
        out_ref[0:HD, there] = (
            in0[0:HD, there].astype(jnp.float32) * w[0]
            + in1[0:HD, there].astype(jnp.float32) * w[1]
        )
        out_ref[HD:MSG, there] = jnp.concatenate(
            [top, w[0] + w[1], jnp.zeros((6, BLK), jnp.float32)], axis=0
        )


def fold_kernel(joined, in0, in1, out_ref):
    def dest(s, e):
        return 16 * ((lax.axis_index("xh") + (e >> 2)) & 1) + 8 * (e & 1) + 2 * s + ((e >> 1) & 1)

    for s in range(SEQS):
        tails = []
        for h in range(HEADS):
            unit = s * HEADS + h
            there = slice(unit * BLK, (unit + 1) * BLK)
            logs = [joined[HD:HD + 1, there], logs_of(in0, there), logs_of(in1, there)]
            top = functools.reduce(jnp.maximum, logs)
            w = [jnp.exp2(x - top) for x in logs]
            total = joined[HD + 1:HD + 2, there] * w[0] + w[1] + w[2]
            inv = 1.0 / total
            ctx = (
                joined[0:HD, there] * (w[0] * inv)
                + in0[0:HD, there].astype(jnp.float32) * (w[1] * inv)
                + in1[0:HD, there].astype(jnp.float32) * (w[2] * inv)
            )
            ctx = jnp.transpose(ctx).astype(jnp.bfloat16)
            for e in range(8):
                out_ref[dest(s, e), h * GROUP:(h + 1) * GROUP, :] = ctx[e * GROUP:(e + 1) * GROUP]
            tails.extend(split3(top + jnp.log(total) * LOG2E))
        tail = jnp.concatenate(tails + [jnp.zeros((2, BLK), jnp.float32)], axis=0)
        for e in range(8):
            turned = tail if e == 0 else pltpu.roll(tail, BLK - GROUP * e, 1)
            out_ref[dest(s, e), 32:LAST, :] = turned.astype(jnp.bfloat16)


def finish_kernel(in_ref, out_ref):
    for kvh in range(2):
        sources = [16 * xh + 8 * kvh + z for xh in range(2) for z in range(8)]
        t = jnp.concatenate(
            [in_ref[n, 32:LAST, :].astype(jnp.float32) for n in sources], axis=0
        )
        t = jnp.transpose(t)[0:GROUP]
        cols = t + pltpu.roll(t, BLK - 1, 1) + pltpu.roll(t, BLK - 2, 1)
        for h in range(HEADS):
            logs = []
            for n in range(16):
                at = n * 8 + 3 * h
                logs.append(jnp.broadcast_to(cols[:, at:at + 1], (GROUP, HD)))
            top = functools.reduce(jnp.maximum, logs)
            total = jnp.zeros((GROUP, HD), jnp.float32)
            ctx = jnp.zeros((GROUP, HD), jnp.float32)
            for n in range(16):
                w = jnp.exp2(logs[n] - top)
                total = total + w
                ctx = ctx + w * in_ref[
                    sources[n], h * GROUP:(h + 1) * GROUP, :
                ].astype(jnp.float32)
            first = kvh * 32 + h * GROUP
            out_ref[0, first:first + GROUP, :] = (ctx / total).astype(jnp.bfloat16)


def turn(x, axis, size, step):
    return lax.ppermute(x, axis, [((i + step) % size, i) for i in range(size)])


def params(mib):
    return pltpu.CompilerParams(vmem_limit_bytes=mib << 20)


def by_head(x):
    return jnp.transpose(x.reshape(OWN * BLK, HEADS, HD), (1, 0, 2))


def per_device(queries, k_cache, v_cache, block_owner, cached_lens, new_counts):
    k0, v0 = (x.reshape(OWN * WIDE, HD) for x in (k_cache, v_cache))
    k1, v1, ids = (turn(x, "core", 2, 1) for x in (k0, v0, block_owner))

    lists = pl.pallas_call(
        select_kernel,
        out_shape=jax.ShapeDtypeStruct((3, 32), jnp.int32),
        in_specs=[SMEM],
        out_specs=SMEM,
        compiler_params=params(12),
        name="select",
    )(jnp.concatenate([block_owner, ids, cached_lens, new_counts]))

    q = jnp.broadcast_to(queries[None], (8,) + queries.shape)
    q = lax.all_to_all(q, "z", split_axis=0, concat_axis=0, tiled=True)
    k0, v0 = by_head(k0), by_head(v0)
    q, lists, k0, k1, v0, v1 = lax.optimization_barrier((q, lists, k0, k1, v0, v1))
    k1, v1 = by_head(k1), by_head(v1)
    k, v = pl.pallas_call(
        pack_kernel,
        out_shape=[
            jax.ShapeDtypeStruct((PAIRS, HEADS, 2 * BLK, HD), jnp.bfloat16),
            jax.ShapeDtypeStruct((PAIRS, HEADS, HD, 2 * BLK), jnp.bfloat16),
        ],
        in_specs=[SMEM] + [VMEM] * 4,
        out_specs=[VMEM, VMEM],
        compiler_params=params(12),
        cost_estimate=COST,
        name="pack",
    )(lists, k0, k1, v0, v1)
    over, k, v = lax.optimization_barrier((turn(q, "xh", 2, 1), k, v))
    near, back = lax.optimization_barrier((turn(q, "y", 4, 1), turn(q, "y", 4, 3)))
    near, back = [near, turn(over, "y", 4, 1)], [back, turn(over, "y", 4, 3)]
    qs = [[q, over], near, [turn(near[0], "y", 4, 1), turn(back[1], "y", 4, 3)], back]

    def attend(*steps):
        n = len(steps)
        rows = n * BLK
        return pl.pallas_call(
            functools.partial(attend_kernel, steps),
            out_shape=[jax.ShapeDtypeStruct((MSG, 8 * BLK), jnp.bfloat16)] * n,
            in_specs=[SMEM] * 3 + [VMEM] * (2 * n + 2),
            out_specs=[VMEM] * n,
            scratch_shapes=[
                pltpu.VMEM((UNITS, 8, rows), jnp.float32),
                pltpu.VMEM((UNITS, 8, rows), jnp.float32),
                pltpu.VMEM((UNITS, HD, rows), jnp.float32),
                pltpu.VMEM((PAIRS, HEADS, 2 * BLK, rows), jnp.float32),
            ],
            compiler_params=params(12),
            cost_estimate=COST,
            name="attend" + "".join(map(str, steps)),
        )(lists, cached_lens, new_counts, *[x for i in steps for x in qs[i]], k, v)

    msg1, msg3 = attend(1, 3)
    (msg2,) = attend(2)
    (msg0,) = attend(0)
    joined = pl.pallas_call(
        join_kernel,
        out_shape=jax.ShapeDtypeStruct((MSG, 8 * BLK), jnp.float32),
        in_specs=[VMEM] * 2,
        out_specs=VMEM,
        compiler_params=params(12),
        cost_estimate=COST,
        name="join",
    )(turn(msg1, "y", 4, -1), turn(msg3, "y", 4, -3))
    msg = pl.pallas_call(
        fold_kernel,
        out_shape=jax.ShapeDtypeStruct((32, LAST, HD), jnp.bfloat16),
        in_specs=[VMEM] * 3,
        out_specs=VMEM,
        compiler_params=params(12),
        name="fold",
    )(joined, msg0, turn(msg2, "y", 4, -2))
    msg = lax.all_to_all(msg, ("xh", "kvh", "z"), split_axis=0, concat_axis=0, tiled=True)
    return pl.pallas_call(
        finish_kernel,
        out_shape=jax.ShapeDtypeStruct((1, 64, HD), jnp.bfloat16),
        in_specs=[VMEM],
        out_specs=VMEM,
        compiler_params=params(12),
        name="finish",
    )(msg)


def solution(mesh):
    split = Mesh(mesh.devices.reshape(8, 4, 2, 2, 2), ("z", "y", "xh", "core", "kvh"))
    ctx = ("z", "y", "xh", "core")
    in_specs = (
        P(ctx, "kvh", None, None),
        P(ctx, "kvh", None),
        P(ctx, "kvh", None),
        P(ctx),
        P(),
        P(),
    )
    return jax.shard_map(
        per_device,
        mesh=split,
        in_specs=in_specs,
        out_specs=P(ctx + ("kvh",), None, None),
        check_vma=False,
    )
```

```python
import functools

import jax
import jax.numpy as jnp
from jax import lax
from jax.experimental import pallas as pl
from jax.experimental.pallas import tpu as pltpu
from jax.sharding import Mesh, PartitionSpec as P

LOG2E = 1.4426950408889634
FLOOR = -1e29
MASKED = -1e30

BLK = 128
OWN = 12
BOTH = 2 * OWN
HEADS = 2
GROUP = 16
HD = 128
SEQS = 4
UNITS = SEQS * HEADS
MSG = HD + 8
BEYOND = 1 << 20
PAIRS = (BOTH + SEQS) // 2
WIDE = HEADS * BLK
LAST = HEADS * GROUP + 8
SMEM = pl.BlockSpec(memory_space=pltpu.SMEM)
VMEM = pl.BlockSpec(memory_space=pltpu.VMEM)
COST = pl.CostEstimate(flops=1_000_000_000, bytes_accessed=4 << 20, transcendentals=0)


def split3(x):
    hi = x.astype(jnp.bfloat16).astype(jnp.float32)
    rest = x - hi
    mid = rest.astype(jnp.bfloat16).astype(jnp.float32)
    return hi, mid, rest - mid


def select_kernel(meta, list_ref):
    blocks_per_seq = (BOTH * 64) // SEQS
    found = []
    for b in range(BOTH):
        ident = meta[b]
        s = sum((ident >= n * blocks_per_seq).astype(jnp.int32) for n in range(1, SEQS))
        number = ident - s * blocks_per_seq
        found.append((s, number, number * BLK <= meta[BOTH + s] + meta[BOTH + SEQS + s] - 1))
    at = []
    end = jnp.int32(0)
    for n in range(SEQS):
        at.append(end)
        here = sum(((s == n) & hit).astype(jnp.int32) for s, _, hit in found)
        end = end + ((here + 1) & -2)
    pairs = ((end >> 1) + 1) & -2
    for e in range(2 * PAIRS):
        list_ref[0, e] = 0
        list_ref[1, e] = BEYOND
    for p in range(PAIRS):
        list_ref[2, p] = sum((p >= (at[n] >> 1)).astype(jnp.int32) for n in range(1, SEQS))
    for n in range(SEQS):
        list_ref[2, 16 + n] = at[n]
    for b, (s, number, hit) in enumerate(found):
        e = jnp.where(hit, list_ref[2, 16 + s], 31)
        list_ref[0, e] = b
        list_ref[1, e] = number
        list_ref[2, 16 + s] += hit.astype(jnp.int32)
    list_ref[2, 31] = pairs


def pack_kernel(lists, k0, k1, v0, v1, k_ref, v_ref):
    def place_pair(p, _):
        for i in range(2):
            here = slice(i * BLK, (i + 1) * BLK)
            b = lists[0, 2 * p + i]

            def put(k_from, v_from, first):
                rows = pl.ds(pl.multiple_of((b - first) * BLK, BLK), BLK)
                for h in range(HEADS):
                    k_ref[p, h, here, :] = k_from[h, rows, :]
                    v_ref[p, h, :, here] = jnp.transpose(v_from[h, rows, :])

            pl.when(b < OWN)(lambda: put(k0, v0, 0))
            pl.when(b >= OWN)(lambda: put(k1, v1, OWN))
        return 0

    lax.fori_loop(0, lists[2, 31], place_pair, 0)


def attend_kernel(steps, *refs):
    n = len(steps)
    lists, cached, counts = refs[:3]
    q_refs, (k_ref, v_ref) = refs[3:3 + 2 * n], refs[3 + 2 * n:5 + 2 * n]
    out_refs, (m_ref, l_ref, acc_ref, t_ref) = refs[5 + 2 * n:5 + 3 * n], refs[5 + 3 * n:]
    rows = BLK * n
    lane = lax.broadcasted_iota(jnp.int32, (1, rows), 1)
    far = steps[0] if n == 1 else jnp.where(lane < BLK, steps[0], steps[1])
    within = (
        32 * ((lane >> 5) & 1)
        + 8 * ((lax.axis_index("y") + far) & 3)
        + 4 * (((lane >> 6) + lax.axis_index("xh")) & 1)
        + 2 * lax.axis_index("core")
        + ((lane >> 4) & 1)
    )
    slot = lax.broadcasted_iota(jnp.int32, (BLK, rows), 0)
    scale = LOG2E * HD ** -0.5
    count = lists[2, 31]
    m_ref[...] = jnp.full(m_ref.shape, FLOOR, jnp.float32)
    l_ref[...] = jnp.zeros(l_ref.shape, jnp.float32)
    acc_ref[...] = jnp.zeros(acc_ref.shape, jnp.float32)

    def score(j, _):
        for p in (2 * j, 2 * j + 1):
            s = lists[2, p]
            qpos = jnp.where(within < counts[s], cached[s] + within, -1)
            for h in range(HEADS):
                unit = s * HEADS + h
                q = jnp.concatenate(
                    [r[pl.ds(2 * s, 2), :, h].reshape(BLK // 2, HD) for r in q_refs], axis=0
                )
                t = lax.dot_general(
                    k_ref[p, h], q, (((1,), (1,)), ((), ())), preferred_element_type=jnp.float32
                )
                top = None
                for i in range(2):
                    limit = qpos - lists[1, 2 * p + i] * BLK
                    part = jnp.where(slot <= limit, t[i * BLK:(i + 1) * BLK] * scale, MASKED)
                    t_ref[p, h, i * BLK:(i + 1) * BLK, :] = part
                    peak = jnp.max(part.reshape(BLK // 8, 8, rows), axis=0)
                    top = peak if top is None else jnp.maximum(top, peak)
                m_ref[unit] = jnp.maximum(m_ref[unit], top)
        return 0

    lax.fori_loop(0, count >> 1, score, 0)
    for unit in range(UNITS):
        m_ref[unit] = jnp.broadcast_to(
            jnp.max(m_ref[unit], axis=0, keepdims=True), (8, rows)
        )

    def weigh(j, _):
        for p in (2 * j, 2 * j + 1):
            s = lists[2, p]
            for h in range(HEADS):
                unit = s * HEADS + h
                w = jnp.exp2(t_ref[p, h].reshape(2 * BLK // 8, 8, rows) - m_ref[unit][None])
                l_ref[unit] += jnp.sum(w, axis=0)
                acc_ref[unit] += jnp.dot(
                    v_ref[p, h],
                    w.reshape(2 * BLK, rows).astype(jnp.bfloat16),
                    preferred_element_type=jnp.float32,
                )
        return 0

    lax.fori_loop(0, count >> 1, weigh, 0)

    for unit in range(UNITS):
        total = jnp.sum(l_ref[unit], axis=0, keepdims=True)
        some = total > 0.0
        safe = jnp.where(some, total, 1.0)
        lse = jnp.where(some, m_ref[unit, 0:1, :] + jnp.log(safe) * LOG2E, MASKED)
        ctx = acc_ref[unit] * (1.0 / safe)
        tail = jnp.concatenate(split3(lse) + (jnp.zeros((5, rows), jnp.float32),), axis=0)
        for i, out_ref in enumerate(out_refs):
            cols = slice(i * BLK, (i + 1) * BLK)
            there = slice(unit * BLK, (unit + 1) * BLK)
            out_ref[0:HD, there] = ctx[:, cols].astype(jnp.bfloat16)
            out_ref[HD:MSG, there] = tail[:, cols].astype(jnp.bfloat16)


def logs_of(ref, there):
    t = ref[HD:MSG, there].astype(jnp.float32)
    return t[0:1] + t[1:2] + t[2:3]


def join_kernel(in0, in1, out_ref):
    for unit in range(UNITS):
        there = slice(unit * BLK, (unit + 1) * BLK)
        logs = [logs_of(r, there) for r in (in0, in1)]
        top = jnp.maximum(*logs)
        w = [jnp.exp2(x - top) for x in logs]
        out_ref[0:HD, there] = (
            in0[0:HD, there].astype(jnp.float32) * w[0]
            + in1[0:HD, there].astype(jnp.float32) * w[1]
        )
        out_ref[HD:MSG, there] = jnp.concatenate(
            [top, w[0] + w[1], jnp.zeros((6, BLK), jnp.float32)], axis=0
        )


def fold_kernel(joined, in0, in1, out_ref):
    def dest(s, e):
        return 8 * s + 4 * ((e >> 1) & 1) + 2 * ((lax.axis_index("xh") + (e >> 2)) & 1) + (e & 1)

    for s in range(SEQS):
        tails = []
        for h in range(HEADS):
            unit = s * HEADS + h
            there = slice(unit * BLK, (unit + 1) * BLK)
            logs = [joined[HD:HD + 1, there], logs_of(in0, there), logs_of(in1, there)]
            top = functools.reduce(jnp.maximum, logs)
            w = [jnp.exp2(x - top) for x in logs]
            total = joined[HD + 1:HD + 2, there] * w[0] + w[1] + w[2]
            inv = 1.0 / total
            ctx = (
                joined[0:HD, there] * (w[0] * inv)
                + in0[0:HD, there].astype(jnp.float32) * (w[1] * inv)
                + in1[0:HD, there].astype(jnp.float32) * (w[2] * inv)
            )
            ctx = jnp.transpose(ctx).astype(jnp.bfloat16)
            for e in range(8):
                out_ref[dest(s, e), h * GROUP:(h + 1) * GROUP, :] = ctx[e * GROUP:(e + 1) * GROUP]
            tails.extend(split3(top + jnp.log(total) * LOG2E))
        tail = jnp.concatenate(tails + [jnp.zeros((2, BLK), jnp.float32)], axis=0)
        for e in range(8):
            turned = tail if e == 0 else pltpu.roll(tail, BLK - GROUP * e, 1)
            out_ref[dest(s, e), 32:LAST, :] = turned.astype(jnp.bfloat16)


def finish_kernel(in_ref, out_ref):
    for kvh in range(2):
        sources = [2 * n + kvh for n in range(16)]
        t = jnp.concatenate(
            [in_ref[n, 32:LAST, :].astype(jnp.float32) for n in sources], axis=0
        )
        t = jnp.transpose(t)[0:GROUP]
        cols = t + pltpu.roll(t, BLK - 1, 1) + pltpu.roll(t, BLK - 2, 1)
        for h in range(HEADS):
            logs = []
            for n in range(16):
                at = n * 8 + 3 * h
                logs.append(jnp.broadcast_to(cols[:, at:at + 1], (GROUP, HD)))
            top = functools.reduce(jnp.maximum, logs)
            total = jnp.zeros((GROUP, HD), jnp.float32)
            ctx = jnp.zeros((GROUP, HD), jnp.float32)
            for n in range(16):
                w = jnp.exp2(logs[n] - top)
                total = total + w
                ctx = ctx + w * in_ref[
                    sources[n], h * GROUP:(h + 1) * GROUP, :
                ].astype(jnp.float32)
            first = kvh * 32 + h * GROUP
            out_ref[0, first:first + GROUP, :] = (ctx / total).astype(jnp.bfloat16)


def turn(x, axis, size, step):
    return lax.ppermute(x, axis, [((i + step) % size, i) for i in range(size)])


def params(mib):
    return pltpu.CompilerParams(vmem_limit_bytes=mib << 20)


def by_head(x):
    return jnp.transpose(x.reshape(OWN * BLK, HEADS, HD), (1, 0, 2))


def per_device(queries, k_cache, v_cache, block_owner, cached_lens, new_counts):
    k0, v0 = (x.reshape(OWN * WIDE, HD) for x in (k_cache, v_cache))
    k1, v1, ids = (turn(x, "core", 2, 1) for x in (k0, v0, block_owner))

    lists = pl.pallas_call(
        select_kernel,
        out_shape=jax.ShapeDtypeStruct((3, 32), jnp.int32),
        in_specs=[SMEM],
        out_specs=SMEM,
        compiler_params=params(12),
        name="select",
    )(jnp.concatenate([block_owner, ids, cached_lens, new_counts]))

    q = jnp.broadcast_to(queries[None], (8,) + queries.shape)
    q = lax.all_to_all(q, "z", split_axis=0, concat_axis=0, tiled=True)
    k0, v0 = by_head(k0), by_head(v0)
    q, lists, k0, k1, v0, v1 = lax.optimization_barrier((q, lists, k0, k1, v0, v1))
    k1, v1 = by_head(k1), by_head(v1)
    k, v = pl.pallas_call(
        pack_kernel,
        out_shape=[
            jax.ShapeDtypeStruct((PAIRS, HEADS, 2 * BLK, HD), jnp.bfloat16),
            jax.ShapeDtypeStruct((PAIRS, HEADS, HD, 2 * BLK), jnp.bfloat16),
        ],
        in_specs=[SMEM] + [VMEM] * 4,
        out_specs=[VMEM, VMEM],
        compiler_params=params(12),
        cost_estimate=COST,
        name="pack",
    )(lists, k0, k1, v0, v1)
    over, k, v = lax.optimization_barrier((turn(q, "xh", 2, 1), k, v))
    near, back = lax.optimization_barrier((turn(q, "y", 4, 1), turn(q, "y", 4, 3)))
    near, back = [near, turn(over, "y", 4, 1)], [back, turn(over, "y", 4, 3)]
    qs = [[q, over], near, [turn(near[0], "y", 4, 1), turn(over, "y", 4, 2)], back]

    def attend(*steps):
        n = len(steps)
        rows = n * BLK
        return pl.pallas_call(
            functools.partial(attend_kernel, steps),
            out_shape=[jax.ShapeDtypeStruct((MSG, 8 * BLK), jnp.bfloat16)] * n,
            in_specs=[SMEM] * 3 + [VMEM] * (2 * n + 2),
            out_specs=[VMEM] * n,
            scratch_shapes=[
                pltpu.VMEM((UNITS, 8, rows), jnp.float32),
                pltpu.VMEM((UNITS, 8, rows), jnp.float32),
                pltpu.VMEM((UNITS, HD, rows), jnp.float32),
                pltpu.VMEM((PAIRS, HEADS, 2 * BLK, rows), jnp.float32),
            ],
            compiler_params=params(12),
            cost_estimate=COST,
            name="attend" + "".join(map(str, steps)),
        )(lists, cached_lens, new_counts, *[x for i in steps for x in qs[i]], k, v)

    msg1, msg3 = attend(1, 3)
    (msg2,) = attend(2)
    (msg0,) = attend(0)
    joined = pl.pallas_call(
        join_kernel,
        out_shape=jax.ShapeDtypeStruct((MSG, 8 * BLK), jnp.float32),
        in_specs=[VMEM] * 2,
        out_specs=VMEM,
        compiler_params=params(12),
        cost_estimate=COST,
        name="join",
    )(turn(msg1, "y", 4, -1), turn(msg3, "y", 4, -3))
    msg = pl.pallas_call(
        fold_kernel,
        out_shape=jax.ShapeDtypeStruct((32, LAST, HD), jnp.bfloat16),
        in_specs=[VMEM] * 3,
        out_specs=VMEM,
        compiler_params=params(12),
        name="fold",
    )(joined, msg0, turn(msg2, "y", 4, -2))
    msg = lax.all_to_all(msg, ("z", "xh", "kvh"), split_axis=0, concat_axis=0, tiled=True)
    return pl.pallas_call(
        finish_kernel,
        out_shape=jax.ShapeDtypeStruct((1, 64, HD), jnp.bfloat16),
        in_specs=[VMEM],
        out_specs=VMEM,
        compiler_params=params(12),
        name="finish",
    )(msg)


def solution(mesh):
    split = Mesh(mesh.devices.reshape(8, 4, 2, 2, 2), ("z", "y", "xh", "core", "kvh"))
    ctx = ("z", "y", "xh", "core")
    in_specs = (
        P(ctx, "kvh", None, None),
        P(ctx, "kvh", None),
        P(ctx, "kvh", None),
        P(ctx),
        P(),
        P(),
    )
    return jax.shard_map(
        per_device,
        mesh=split,
        in_specs=in_specs,
        out_specs=P(ctx + ("kvh",), None, None),
        check_vma=False,
    )
```
